512 devices in a mesh: row: 16 (over x, z_lo, core), col: 32 (over z_hi, y).
Axes of the slice: x: 4, y: 8, z: 8 (z_hi: 4, z_lo: 2; z = z_hi * 2 + z_lo), core: 2. Of those that a mesh axis runs over, the one named last changes fastest.
Arguments:
- val_orbitals: bfloat16 [48, 64, 4096], P(None, 'col'), may hold values from -6 to 6
- cond_orbitals: bfloat16 [64, 64, 4096], P(None, 'col'), may hold values from -6 to 6
- val_index: int32 [1024], replicated, may hold values from 0 to 47
- cond_index: int32 [1024], replicated, may hold values from 0 to 63
- val_energy: float32 [48], replicated, may hold values from -12 to -2
- cond_energy: float32 [64], replicated, may hold values from 0.5 to 15
- freqs: float32 [2], replicated, may hold values from 0.5 to 20
- gmap: int32 [12288], replicated, may hold values from 1 to 524255, as said below
Outputs:
- chi_zero: float32 [2, 12288, 12288], P(None, 'row', 'col')
The draws below stay inside these ranges and needn't reach their ends.
Inputs may be any that keep to these rules, and one draw needn't show every extreme that they name: `gmap`: the entries are distinct. Each is ((part * 64 + a) * 64 + q) * 64 + k with part 0 or 1, a and q below 64 and 1 <= k < 32; (a, q, k) lies among the 12288 such wave vectors nearest to zero, length measured with a and q read as a - 64 and q - 64 when they are 32 or more (ties broken by the order of ((a * 64 + q) * 64 + k)); a wave vector present with part 0 is present with part 1 too.
All inputs are finite; a program needn't handle non-finite values.
Results may differ from the reference program's by a relative error of at most 0.0099.
Values may be sent and summed in bfloat16 or wider, within the bound.
No kernel may reach another device: no remote copies, remote signals or barrier semaphores. Data moves between devices by JAX's collectives and lax.ppermute only.
A program may use at most 64 MiB of HBM per device.

```python
import math
import jax
import jax.numpy as jnp
import numpy as np
from jax import lax

NVAL = 48
NCOND = 64
GRID = 64
NG = 12288
NFREQ = 2
PAIR_DEV = 64
PAIRS = 1024


def draw_gmap(key, part):
    key = jax.random.fold_in(key, 7)
    half_grid = GRID // 2
    axis_vals = np.arange(GRID)
    signed = np.where(axis_vals < half_grid, axis_vals, axis_vals - GRID)
    wave_a, wave_q, wave_k = np.meshgrid(axis_vals, axis_vals, np.arange(1, half_grid), indexing='ij')
    lengths = signed[wave_a] ** 2 + signed[wave_q] ** 2 + wave_k ** 2
    flat_index = (wave_a * GRID + wave_q) * GRID + wave_k
    ranking = np.argsort(lengths.ravel(), kind='stable')
    nearest = jnp.asarray(flat_index.ravel()[ranking[:NG]].astype(np.int32))
    first_key, second_key = jax.random.split(key)
    chosen = nearest[jax.random.permutation(first_key, NG)[:NG // 2]]
    entries = jnp.concatenate([chosen, chosen + GRID * GRID * GRID])
    return entries[jax.random.permutation(second_key, NG)].astype(jnp.int32)


def touch_ends(drawn, rng, smallest, top_value):
    shape = drawn.shape
    spot = [jax.random.randint(jax.random.fold_in(rng, axis), (), 0, shape[axis]) for axis in range(len(shape))]
    drawn = drawn.at[tuple(spot)].set(smallest)
    longest = shape.index(max(shape))
    spot[longest] = (spot[longest] + 1) % shape[longest]
    return drawn.at[tuple(spot)].set(top_value)


def shard_levels(rng, extent, shards, smallest, top_value):
    gain = 1.0
    for position, parts in shards:
        draws = jax.random.uniform(jax.random.fold_in(jax.random.fold_in(rng, 6), position), (parts,), jnp.float32, smallest / len(shards), top_value / len(shards))
        gain = gain * jnp.repeat(jnp.exp(draws), extent[position] // parts).reshape((-1,) + (1,) * (len(extent) - 1 - position))
    return gain


def normal_values(stream_key, extent, scale, limit, cuts=(), held_as=jnp.bfloat16):
    gain = shard_levels(stream_key, extent, cuts, -0.22, 0.18) if cuts else 1.0
    drawn = jax.random.normal(stream_key, extent, jnp.float32) * scale * gain
    return jnp.minimum(jnp.maximum(drawn, -limit), limit).astype(held_as)


def setup_inputs(seed: int = 0) -> dict:
    streams_of = jax.random.split(jax.random.key(seed), 9)
    val_orbitals = normal_values(streams_of[0], (NVAL, GRID, GRID * GRID), 1.0, 6.0, ((1, 32),))
    cond_orbitals = normal_values(streams_of[1], (NCOND, GRID, GRID * GRID), 1.0, 6.0, ((1, 32),))
    val_index = touch_ends(jax.random.randint(streams_of[2], (PAIRS,), 0, NVAL), jax.random.fold_in(streams_of[2], 1), 0, NVAL - 1).astype(jnp.int32)
    cond_index = touch_ends(jax.random.randint(streams_of[3], (PAIRS,), 0, NCOND), jax.random.fold_in(streams_of[3], 1), 0, NCOND - 1).astype(jnp.int32)
    val_energy = jnp.clip(jax.random.uniform(streams_of[4], (NVAL,), jnp.float32, -12.0, -2.0), -12.0, -2.0)
    cond_energy = jnp.clip(jax.random.uniform(streams_of[5], (NCOND,), jnp.float32, 0.5, 15.0), 0.5, 15.0)
    freqs = jnp.clip(jnp.exp(jax.random.uniform(streams_of[6], (NFREQ,), jnp.float32, math.log(0.5), math.log(20.0))), 0.5, 20.0)
    gmap = draw_gmap(jax.random.fold_in(streams_of[8], 71), 0)
    return dict(val_orbitals=val_orbitals, cond_orbitals=cond_orbitals, val_index=val_index, cond_index=cond_index, val_energy=val_energy, cond_energy=cond_energy, freqs=freqs, gmap=gmap)


def dft_tables(length, count):
    rows_iota = jnp.arange(length, dtype=jnp.int32)[:, None]
    cols_iota = jnp.arange(count, dtype=jnp.int32)[None, :]
    phase = (rows_iota * cols_iota % length).astype(jnp.float32) * (2.0 * math.pi / length)
    return (jnp.cos(phase).astype(jnp.bfloat16), jnp.sin(phase).astype(jnp.bfloat16))

def reference(val_orbitals, cond_orbitals, val_index, cond_index, val_energy, cond_energy, freqs, gmap):
    half_grid = GRID // 2
    cos_full, sin_full = dft_tables(GRID, GRID)
    cos_half, sin_half = dft_tables(GRID, half_grid)
    z_table = jnp.concatenate([cos_half, -sin_half], 1).astype(jnp.float32)
    cos_y = cos_full.astype(jnp.float32)
    sin_y = sin_full.astype(jnp.float32)
    cube = GRID * GRID * GRID
    part_of = gmap // cube
    remain = gmap % cube
    wave_a = remain // (GRID * GRID)
    wave_q = remain // GRID % GRID
    wave_k = remain % GRID
    flat_index = ((wave_a * GRID + wave_q) * GRID + part_of * half_grid + wave_k).astype(jnp.int32)
    scale_grid = float(GRID) ** (-1.5)
    high = lax.Precision.HIGHEST

    def pair_block(indices):
        val_rows, cond_rows = indices
        density = (jnp.take(val_orbitals, val_rows, axis=0).astype(jnp.float32) * jnp.take(cond_orbitals, cond_rows, axis=0).astype(jnp.float32)).astype(jnp.bfloat16)
        density = density.astype(jnp.float32).reshape(density.shape[0], GRID, GRID, GRID)
        z_partial = jnp.einsum('bxyz,zk->bxyk', density, z_table, precision=high).astype(jnp.bfloat16).astype(jnp.float32)
        with_cos = jnp.einsum('bxyk,yq->bxqk', z_partial, cos_y, precision=high)
        with_sin = jnp.einsum('bxyk,yq->bxqk', z_partial, sin_y, precision=high)
        y_partial = jnp.concatenate([with_cos[..., :half_grid] + with_sin[..., half_grid:], with_cos[..., half_grid:] - with_sin[..., :half_grid]], -1).astype(jnp.bfloat16).astype(jnp.float32)
        x_cos = jnp.einsum('bxqk,xa->baqk', y_partial, cos_y, precision=high)
        x_sin = jnp.einsum('bxqk,xa->baqk', y_partial, sin_y, precision=high)
        spectrum = jnp.concatenate([x_cos[..., :half_grid] + x_sin[..., half_grid:], x_cos[..., half_grid:] - x_sin[..., :half_grid]], -1)
        flat_spec = spectrum.reshape(spectrum.shape[0], -1)
        return (jnp.take(flat_spec, flat_index, axis=1) * scale_grid).astype(jnp.bfloat16)
    block_count = val_index.shape[0] // PAIR_DEV
    packed = lax.map(pair_block, (val_index.reshape(block_count, PAIR_DEV), cond_index.reshape(block_count, PAIR_DEV)))
    pair_matrix = packed.reshape(val_index.shape[0], NG).T
    gap = jnp.take(cond_energy, cond_index) - jnp.take(val_energy, val_index)
    weight = -4.0 * gap[None, :] / (gap[None, :] ** 2 + freqs[:, None] ** 2)
    matrix_f = pair_matrix.astype(jnp.float32)
    weighted = (weight[:, None, :] * matrix_f[None]).astype(jnp.bfloat16)
    scale = 1.0 / math.sqrt(val_index.shape[0])
    chi_zero = jnp.einsum('fgp,hp->fgh', weighted.astype(jnp.float32), matrix_f, precision=high)
    return chi_zero * scale
```

```python
import functools
import math

import jax
import jax.numpy as jnp
import numpy as np
from jax import lax
from jax.experimental import pallas as pl
from jax.experimental.pallas import tpu as pltpu
from jax.sharding import Mesh, PartitionSpec as P

GRID = 64
NG = 12288
REACH = 18
SIDE = 2 * REACH + 1
RADIUS2 = 334
COLS = 512
PAIR_ROWS = 80
TILE = 128
BF16 = jnp.bfloat16
F32 = jnp.float32


def tables():
    idx = np.arange(GRID)
    phase = (idx[:, None] * idx[None, :] % GRID).astype(np.float32) * np.float32(2.0 * math.pi / GRID)
    phase = phase.astype(np.float64)
    return np.cos(phase), np.sin(phase)


def columns():
    found = []
    for k in range(1, REACH + 1):
        for q in range(-REACH, REACH + 1):
            if q * q + k * k <= RADIUS2:
                found.append((q % GRID, k))
    return found


def z_constant():
    cos, sin = tables()
    out = np.zeros((REACH, 4, 2, 4, GRID), np.float64)
    for k in range(1, REACH + 1):
        for y in range(4):
            out[k - 1, y, 0, y] = cos[:, k]
            out[k - 1, y, 1, y] = -sin[:, k]
    return out.reshape(REACH * 8, 4 * GRID)


def y_spans():
    cols = columns()
    spans = []
    for start in range(0, COLS, TILE):
        ks = [k for _, k in cols[start : start + TILE]]
        spans.append((min(ks) - 1, max(ks)))
    return spans


def y_constant():
    cos, sin = tables()
    cols = columns()
    blocks = []
    for tile, (first, last) in enumerate(y_spans()):
        block = np.zeros((last - first, GRID, 2, 2, TILE), np.float64)
        for lane, (q, k) in enumerate(cols[tile * TILE : (tile + 1) * TILE]):
            block[k - 1 - first, :, 0, 0, lane] = cos[:, q]
            block[k - 1 - first, :, 1, 0, lane] = sin[:, q]
            block[k - 1 - first, :, 0, 1, lane] = -sin[:, q]
            block[k - 1 - first, :, 1, 1, lane] = cos[:, q]
        blocks.append(block.reshape(-1, 2 * TILE))
    return np.concatenate(blocks, 0)


def x_constant():
    cos, sin = tables()
    out = np.zeros((2, PAIR_ROWS, GRID // 2, 2, 2, 2), np.float64)
    for pair in range(2):
        for a in range(-REACH, REACH + 1):
            c = cos[:, a % GRID].reshape(-1, 2)
            s = sin[:, a % GRID].reshape(-1, 2)
            out[pair, a + REACH, :, 0, pair] = c
            out[pair, a + REACH, :, 1, pair] = s
            out[pair, SIDE + a + REACH, :, 0, pair] = -s
            out[pair, SIDE + a + REACH, :, 1, pair] = c
    return out.reshape(2 * PAIR_ROWS, 4 * GRID)


def column_keys():
    keys = np.full((COLS, 1), -1, np.int32)
    for lane, (q, k) in enumerate(columns()):
        keys[lane, 0] = q * GRID + k
    return keys


def transform_kernel(vi_ref, ci_ref, val_ref, cond_ref, zt_ref, yt_ref, out_ref, dens_ref, part_ref):
    pairs = dens_ref.shape[0] // 2
    for p in range(pairs):
        dens_ref[2 * p : 2 * p + 2, :] = val_ref[vi_ref[p]] * cond_ref[ci_ref[p]]
    for j in range(GRID // 4):
        zt = lax.dot_general(
            zt_ref[...],
            dens_ref[:, j * 256 : (j + 1) * 256],
            (((1,), (1,)), ((), ())),
            preferred_element_type=F32,
        )
        part_ref[:, j * 8 : (j + 1) * 8, :] = zt.reshape(REACH, 8, 2 * pairs)
    low = lax.broadcasted_iota(jnp.int32, (2 * pairs, TILE), 0) % 8 < 4
    row = 0
    for tile, (first, last) in enumerate(y_spans()):
        depth = (last - first) * 2 * GRID
        left = part_ref[first:last].astype(BF16).reshape(depth, 2 * pairs)
        both = lax.dot_general(
            left, yt_ref[row : row + depth, :], (((0,), (0,)), ((), ())), preferred_element_type=F32
        )
        row += depth
        real, imag = both[:, :TILE], both[:, TILE:]
        even = jnp.where(low, real, pltpu.roll(imag, 4, 0))
        odd = jnp.where(low, pltpu.roll(real, 2 * pairs - 4, 0), imag)
        for m in range(2 * pairs // 8):
            out_ref[16 * m : 16 * m + 16, tile * TILE : (tile + 1) * TILE] = jnp.concatenate(
                [even[8 * m : 8 * m + 8], odd[8 * m : 8 * m + 8]], 0
            ).astype(BF16)


def transform(own_val, own_cond, val_orbitals, cond_orbitals):
    pairs = own_val.shape[0]
    smem = pl.BlockSpec(memory_space=pltpu.SMEM)
    vmem = pl.BlockSpec(memory_space=pltpu.VMEM)
    return pl.pallas_call(
        transform_kernel,
        out_shape=jax.ShapeDtypeStruct((4 * pairs, COLS), BF16),
        in_specs=[smem, smem, vmem, vmem, vmem, vmem],
        out_specs=vmem,
        scratch_shapes=[
            pltpu.VMEM((2 * pairs, GRID * GRID), BF16),
            pltpu.VMEM((REACH, 2 * GRID, 2 * pairs), F32),
        ],
        compiler_params=pltpu.CompilerParams(vmem_limit_bytes=40 * 2**20),
        name="transform",
    )(
        own_val,
        own_cond,
        val_orbitals,
        cond_orbitals,
        jnp.asarray(z_constant(), BF16),
        jnp.asarray(y_constant(), BF16),
    )


def select_kernel(y_ref, xt_ref, key_ref, gmap_ref, g_ref, h_ref, spec_ref):
    @pl.when(pl.program_id(0) == 0)
    def _():
        spec = jnp.dot(xt_ref[...], y_ref[...], preferred_element_type=F32)
        spec_ref[...] = (spec * float(GRID) ** (-1.5)).astype(BF16)

    entry = gmap_ref[0]
    width = entry.shape[1]
    key = entry & (GRID * GRID - 1)
    wave_a = (entry >> 12) & (GRID - 1)
    row = (entry >> 18) * SIDE + ((wave_a + REACH) & (GRID - 1))
    hit = jnp.where(key_ref[...] == key, 1.0, 0.0).astype(BF16)
    found = jnp.dot(spec_ref[...], hit, preferred_element_type=F32)
    rows = lax.broadcasted_iota(jnp.int32, (PAIR_ROWS, width), 0) == row
    picked = [
        jnp.sum(jnp.where(rows, found[i * PAIR_ROWS : (i + 1) * PAIR_ROWS], 0.0), 0, keepdims=True)
        for i in range(2)
    ]
    both = jnp.concatenate(picked, 0).astype(BF16)
    for copy in range(g_ref.shape[0]):
        g_ref[copy] = both
    half = width // 2
    h_ref[0] = both[:, :half]
    h_ref[1] = both[:, half:]


def select(block, gmap, copies, rows):
    width = NG // rows
    return pl.pallas_call(
        select_kernel,
        grid=(rows,),
        out_shape=(
            jax.ShapeDtypeStruct((rows * copies, 2, width), BF16),
            jax.ShapeDtypeStruct((rows * 2, 2, width // 2), BF16),
        ),
        in_specs=[
            pl.BlockSpec((4 * GRID, COLS), lambda i: (0, 0)),
            pl.BlockSpec((2 * PAIR_ROWS, 4 * GRID), lambda i: (0, 0)),
            pl.BlockSpec((COLS, 1), lambda i: (0, 0)),
            pl.BlockSpec((1, 1, width), lambda i: (i, 0, 0)),
        ],
        out_specs=(
            pl.BlockSpec((copies, 2, width), lambda i: (i, 0, 0)),
            pl.BlockSpec((2, 2, width // 2), lambda i: (i, 0, 0)),
        ),
        scratch_shapes=[pltpu.VMEM((2 * PAIR_ROWS, COLS), BF16)],
        compiler_params=pltpu.CompilerParams(
            dimension_semantics=("arbitrary",), vmem_limit_bytes=40 * 2**20
        ),
        name="select",
    )(block, jnp.asarray(x_constant(), BF16), jnp.asarray(column_keys()), gmap.reshape(rows, 1, width))


def pair_weights(val_index, cond_index, val_energy, cond_energy, freqs):
    val_hit = val_index[:, None] == jnp.arange(val_energy.shape[0], dtype=jnp.int32)[None, :]
    cond_hit = cond_index[:, None] == jnp.arange(cond_energy.shape[0], dtype=jnp.int32)[None, :]
    gap = jnp.sum(jnp.where(cond_hit, cond_energy[None, :], 0.0), 1) - jnp.sum(
        jnp.where(val_hit, val_energy[None, :], 0.0), 1
    )
    return -4.0 * gap[None, :] / (gap[None, :] ** 2 + freqs[:, None] ** 2)


ROW = ("x", "z_lo", "core")
COL = ("z_hi", "y")


def reorder(pair_values):
    return pair_values.reshape(16, 4, 8, 2).transpose(2, 0, 1, 3).reshape(-1)


def shards(
    val_orbitals, cond_orbitals, val_index, cond_index, val_energy, cond_energy, freqs, gmap
):
    row_count = lax.axis_size(ROW)
    col_count = lax.axis_size(COL)
    pair_dev = val_index.shape[0] // row_count
    row_index = lax.axis_index(ROW)
    own_val = lax.dynamic_slice_in_dim(val_index, row_index * pair_dev, pair_dev)
    own_cond = lax.dynamic_slice_in_dim(cond_index, row_index * pair_dev, pair_dev)
    partial = transform(own_val, own_cond, val_orbitals, cond_orbitals)
    block = lax.all_to_all(
        partial.reshape(col_count, 8, COLS), COL, split_axis=0, concat_axis=0, tiled=True
    ).reshape(4 * GRID, COLS)
    for_rows, for_cols = select(block, gmap, 4, row_count)
    mine = lax.all_to_all(for_rows, ROW + ("z_hi",), split_axis=0, concat_axis=0, tiled=True)
    mine, for_cols = lax.optimization_barrier((mine, for_cols))
    left = lax.all_gather(mine.reshape(-1, NG // row_count), "y", axis=0, tiled=True)
    width = NG // col_count
    column = lax.all_to_all(for_cols, COL, split_axis=0, concat_axis=0, tiled=True)
    column = column.reshape(4, 8, 2, width).transpose(1, 0, 2, 3).reshape(1, pair_dev, width)
    spread = lax.all_to_all(
        jnp.broadcast_to(column, (row_count, pair_dev, width)), ROW, split_axis=0, concat_axis=0, tiled=True
    )
    right = spread.reshape(row_count, 8, 8, width).transpose(1, 0, 2, 3).reshape(-1, width)
    weights = pair_weights(reorder(val_index), reorder(cond_index), val_energy, cond_energy, freqs)
    weighted = (weights[:, :, None] * left.astype(F32)[None]).astype(BF16)
    product = lax.dot_general(
        weighted, right, (((1,), (0,)), ((), ())), preferred_element_type=F32
    )
    return product * (1.0 / math.sqrt(val_index.shape[0]))


def solution(mesh):
    fine = Mesh(mesh.devices.reshape(4, 2, 2, 4, 8), ROW + COL)
    orbitals = P(None, COL, None)
    placed = (orbitals, orbitals, P(), P(), P(), P(), P(), P())
    return jax.shard_map(
        shards, mesh=fine, in_specs=placed, out_specs=P(None, ROW, COL), check_vma=False
    )
```

```python
import functools
import math

import jax
import jax.numpy as jnp
import numpy as np
from jax import lax
from jax.experimental import pallas as pl
from jax.experimental.pallas import tpu as pltpu
from jax.sharding import Mesh, PartitionSpec as P

GRID = 64
NG = 12288
REACH = 18
SIDE = 2 * REACH + 1
RADIUS2 = 334
COLS = 512
PAIR_ROWS = 80
TILE = 128
CUTS = 1
BF16 = jnp.bfloat16
F32 = jnp.float32
VMEM_LIMIT = 60 * 2**20


def tables():
    idx = np.arange(GRID)
    phase = (idx[:, None] * idx[None, :] % GRID).astype(np.float32) * np.float32(2.0 * math.pi / GRID)
    phase = phase.astype(np.float64)
    return np.cos(phase), np.sin(phase)


def columns():
    found = []
    for k in range(1, REACH + 1):
        for q in range(-REACH, REACH + 1):
            if q * q + k * k <= RADIUS2:
                found.append((q % GRID, k))
    return found


def z_constant():
    cos, sin = tables()
    out = np.zeros((REACH, 4, 2, 4, GRID), np.float64)
    for k in range(1, REACH + 1):
        for y in range(4):
            out[k - 1, y, 0, y] = cos[:, k]
            out[k - 1, y, 1, y] = -sin[:, k]
    return out.reshape(REACH * 8, 4 * GRID)


def y_spans():
    cols = columns()
    spans = []
    for start in range(0, COLS, TILE):
        ks = [k for _, k in cols[start : start + TILE]]
        spans.append((min(ks) - 1, max(ks)))
    return spans


def y_constant():
    cos, sin = tables()
    cols = columns()
    blocks = []
    for tile, (first, last) in enumerate(y_spans()):
        block = np.zeros((last - first, GRID, 2, 2, TILE), np.float64)
        for lane, (q, k) in enumerate(cols[tile * TILE : (tile + 1) * TILE]):
            block[k - 1 - first, :, 0, 0, lane] = cos[:, q]
            block[k - 1 - first, :, 1, 0, lane] = sin[:, q]
            block[k - 1 - first, :, 0, 1, lane] = -sin[:, q]
            block[k - 1 - first, :, 1, 1, lane] = cos[:, q]
        blocks.append(block.reshape(-1, 2 * TILE))
    return np.concatenate(blocks, 0)


def x_constant():
    cos, sin = tables()
    out = np.zeros((2, PAIR_ROWS, GRID // 2, 2, 2, 2), np.float64)
    for pair in range(2):
        for a in range(-REACH, REACH + 1):
            c = cos[:, a % GRID].reshape(-1, 2)
            s = sin[:, a % GRID].reshape(-1, 2)
            out[pair, a + REACH, :, 0, pair] = c
            out[pair, a + REACH, :, 1, pair] = s
            out[pair, SIDE + a + REACH, :, 0, pair] = -s
            out[pair, SIDE + a + REACH, :, 1, pair] = c
    return out.reshape(2 * PAIR_ROWS, 4 * GRID)


def column_keys():
    keys = np.full((COLS, 1), -1, np.int32)
    for lane, (q, k) in enumerate(columns()):
        keys[lane, 0] = q * GRID + k
    return keys


def transform_kernel(
    row_ref, vi_ref, ci_ref, val_hbm, cond_hbm, zt_hbm, yt_hbm, out_ref,
    val_ref, cond_ref, zt_ref, yt_ref, dens_ref, part_ref, sems,
):
    pairs = dens_ref.shape[0] // 2
    moves = []
    for src, dst, parts in (
        (val_hbm, val_ref, CUTS),
        (cond_hbm, cond_ref, CUTS),
        (zt_hbm, zt_ref, 1),
        (yt_hbm, yt_ref, CUTS),
    ):
        size = src.shape[0] // parts
        for part in range(parts):
            cut = pl.ds(part * size, size)
            moves.append(pltpu.make_async_copy(src.at[cut], dst.at[cut], sems.at[len(moves)]))
            moves[-1].start()
    first_pair = row_ref[0] * pairs
    for move in moves[: 2 * CUTS]:
        move.wait()
    for p in range(pairs):
        dens_ref[2 * p : 2 * p + 2, :] = val_ref[vi_ref[first_pair + p]] * cond_ref[ci_ref[first_pair + p]]
    moves[2 * CUTS].wait()
    for j in range(GRID // 4):
        zt = lax.dot_general(
            zt_ref[...],
            dens_ref[:, j * 256 : (j + 1) * 256],
            (((1,), (1,)), ((), ())),
            preferred_element_type=F32,
        )
        part_ref[:, j * 8 : (j + 1) * 8, :] = zt.reshape(REACH, 8, 2 * pairs)
    low = lax.broadcasted_iota(jnp.int32, (2 * pairs, TILE), 0) % 8 < 4
    for move in moves[2 * CUTS + 1 :]:
        move.wait()
    row = 0
    for tile, (first, last) in enumerate(y_spans()):
        depth = (last - first) * 2 * GRID
        left = part_ref[first:last].astype(BF16).reshape(depth, 2 * pairs)
        both = lax.dot_general(
            left, yt_ref[row : row + depth, :], (((0,), (0,)), ((), ())), preferred_element_type=F32
        )
        row += depth
        real, imag = both[:, :TILE], both[:, TILE:]
        even = jnp.where(low, real, pltpu.roll(imag, 4, 0))
        odd = jnp.where(low, pltpu.roll(real, 2 * pairs - 4, 0), imag)
        for m in range(2 * pairs // 8):
            out_ref[16 * m : 16 * m + 16, tile * TILE : (tile + 1) * TILE] = jnp.concatenate(
                [even[8 * m : 8 * m + 8], odd[8 * m : 8 * m + 8]], 0
            ).astype(BF16)


def transform(row_index, pairs, val_index, cond_index, val_orbitals, cond_orbitals):
    smem = pl.BlockSpec(memory_space=pltpu.SMEM)
    hbm = pl.BlockSpec(memory_space=pltpu.HBM)
    z_table, y_table = z_constant(), y_constant()
    return pl.pallas_call(
        transform_kernel,
        out_shape=jax.ShapeDtypeStruct((4 * pairs, COLS), BF16),
        in_specs=[smem, smem, smem, hbm, hbm, hbm, hbm],
        out_specs=pl.BlockSpec(memory_space=pltpu.VMEM),
        scratch_shapes=[
            pltpu.VMEM(val_orbitals.shape, BF16),
            pltpu.VMEM(cond_orbitals.shape, BF16),
            pltpu.VMEM(z_table.shape, BF16),
            pltpu.VMEM(y_table.shape, BF16),
            pltpu.VMEM((2 * pairs, GRID * GRID), BF16),
            pltpu.VMEM((REACH, 2 * GRID, 2 * pairs), F32),
            pltpu.SemaphoreType.DMA((3 * CUTS + 1,)),
        ],
        compiler_params=pltpu.CompilerParams(vmem_limit_bytes=VMEM_LIMIT),
        name="transform",
    )(
        row_index.reshape(1),
        val_index,
        cond_index,
        val_orbitals,
        cond_orbitals,
        jnp.asarray(z_table, BF16),
        jnp.asarray(y_table, BF16),
    )


def select_kernel(y_ref, xt_ref, key_ref, gmap_ref, out_ref):
    spec = jnp.dot(xt_ref[...], y_ref[...], preferred_element_type=F32)
    spec = (spec * float(GRID) ** (-1.5)).astype(BF16)
    rows, _, width = gmap_ref.shape
    copies = out_ref.shape[0] // rows
    side = lax.broadcasted_iota(jnp.int32, (PAIR_ROWS, width), 0)
    for r in range(rows):
        entry = gmap_ref[r]
        key = entry & (GRID * GRID - 1)
        wave_a = (entry >> 12) & (GRID - 1)
        row = (entry >> 18) * SIDE + ((wave_a + REACH) & (GRID - 1))
        hit = jnp.where(key_ref[...] == key, 1.0, 0.0).astype(BF16)
        found = jnp.dot(spec, hit, preferred_element_type=F32)
        here = side == row
        picked = [
            jnp.sum(jnp.where(here, found[i * PAIR_ROWS : (i + 1) * PAIR_ROWS], 0.0), 0, keepdims=True)
            for i in range(2)
        ]
        both = jnp.concatenate(picked, 0).astype(BF16)
        for copy in range(copies):
            out_ref[r * copies + copy] = both


def select(block, gmap, copies, rows):
    width = NG // rows
    vmem = pl.BlockSpec(memory_space=pltpu.VMEM)
    return pl.pallas_call(
        select_kernel,
        out_shape=jax.ShapeDtypeStruct((rows * copies, 2, width), BF16),
        in_specs=[vmem] * 4,
        out_specs=vmem,
        compiler_params=pltpu.CompilerParams(vmem_limit_bytes=40 * 2**20),
        name="select",
    )(block, jnp.asarray(x_constant(), BF16), jnp.asarray(column_keys()), gmap.reshape(rows, 1, width))


def product_kernel(left_ref, right_ref, weight_ref, out_ref):
    turned = left_ref[...].T.astype(F32)
    for f in range(out_ref.shape[0]):
        weighted = (turned * weight_ref[f : f + 1, :]).astype(BF16)
        part = jnp.dot(weighted, right_ref[...], preferred_element_type=F32)
        out_ref[f] = part * (1.0 / math.sqrt(left_ref.shape[0]))


def product(left, right, weights, step=384):
    pairs, rows = left.shape
    width = right.shape[1]
    return pl.pallas_call(
        product_kernel,
        grid=(rows // step,),
        out_shape=jax.ShapeDtypeStruct((weights.shape[0], rows, width), F32),
        in_specs=[
            pl.BlockSpec((pairs, step), lambda i: (0, i)),
            pl.BlockSpec((pairs, width), lambda i: (0, 0)),
            pl.BlockSpec(weights.shape, lambda i: (0, 0)),
        ],
        out_specs=pl.BlockSpec((weights.shape[0], step, width), lambda i: (0, i, 0)),
        compiler_params=pltpu.CompilerParams(
            dimension_semantics=("arbitrary",), vmem_limit_bytes=VMEM_LIMIT
        ),
        name="product",
    )(left, right, weights)


def pair_weights(val_index, cond_index, val_energy, cond_energy, freqs):
    val_hit = val_index[:, None] == jnp.arange(val_energy.shape[0], dtype=jnp.int32)[None, :]
    cond_hit = cond_index[:, None] == jnp.arange(cond_energy.shape[0], dtype=jnp.int32)[None, :]
    gap = jnp.sum(jnp.where(cond_hit, cond_energy[None, :], 0.0), 1) - jnp.sum(
        jnp.where(val_hit, val_energy[None, :], 0.0), 1
    )
    return -4.0 * gap[None, :] / (gap[None, :] ** 2 + freqs[:, None] ** 2)


ROW = ("x", "z_lo", "core")
COL = ("z_hi", "y")


def reorder(pair_values):
    return pair_values.reshape(16, 4, 8, 2).transpose(2, 0, 1, 3).reshape(-1)


def shards(
    val_orbitals, cond_orbitals, val_index, cond_index, val_energy, cond_energy, freqs, gmap
):
    row_count = lax.axis_size(ROW)
    col_count = lax.axis_size(COL)
    pair_dev = val_index.shape[0] // row_count
    partial = transform(
        lax.axis_index(ROW), pair_dev, val_index, cond_index, val_orbitals, cond_orbitals
    )
    block = lax.all_to_all(
        partial.reshape(col_count, 8, COLS), COL, split_axis=0, concat_axis=0, tiled=True
    ).reshape(4 * GRID, COLS)
    for_rows = select(block, gmap, 4, row_count)
    mine = lax.all_to_all(for_rows, ROW + ("z_hi",), split_axis=0, concat_axis=0, tiled=True)
    mine = mine.reshape(-1, NG // row_count)
    left = lax.all_gather(mine, "y", axis=0, tiled=True)
    width = NG // col_count
    z_hi = lax.axis_index("z_hi")
    piece = lax.dynamic_slice(mine, (z_hi // 2 * pair_dev, z_hi % 2 * width), (pair_dev, width))
    column = lax.ppermute(piece, ROW + COL, column_moves())
    right = lax.all_to_all(
        jnp.broadcast_to(column, (row_count, pair_dev, width)), ROW, split_axis=0, concat_axis=0, tiled=True
    ).reshape(-1, width)
    weights = pair_weights(reorder(val_index), reorder(cond_index), val_energy, cond_energy, freqs)
    return product(left, right, weights)


def column_moves():
    moves = []
    for row in range(16):
        for z_hi in range(4):
            for y in range(8):
                moves.append((row * 32 + z_hi * 8 + y, (2 * y + z_hi // 2) * 32 + 2 * row + z_hi % 2))
    return moves


def solution(mesh):
    fine = Mesh(mesh.devices.reshape(4, 2, 2, 4, 8), ROW + COL)
    orbitals = P(None, COL, None)
    placed = (orbitals, orbitals, P(), P(), P(), P(), P(), P())
    return jax.shard_map(
        shards, mesh=fine, in_specs=placed, out_specs=P(None, ROW, COL), check_vma=False
    )
```

```python
import functools
import math

import jax
import jax.numpy as jnp
import numpy as np
from jax import lax
from jax.experimental import pallas as pl
from jax.experimental.pallas import tpu as pltpu
from jax.sharding import Mesh, PartitionSpec as P

GRID = 64
NG = 12288
REACH = 18
SIDE = 2 * REACH + 1
RADIUS2 = 334
COLS = 512
PAIR_ROWS = 80
TILE = 128
CUTS = 1
BF16 = jnp.bfloat16
F32 = jnp.float32
VMEM_LIMIT = 60 * 2**20


def tables():
    idx = np.arange(GRID)
    phase = (idx[:, None] * idx[None, :] % GRID).astype(np.float32) * np.float32(2.0 * math.pi / GRID)
    phase = phase.astype(np.float64)
    return np.cos(phase), np.sin(phase)


def columns():
    found = []
    for k in range(1, REACH + 1):
        for q in range(-REACH, REACH + 1):
            if q * q + k * k <= RADIUS2:
                found.append((q % GRID, k))
    return found


def z_constant():
    cos, sin = tables()
    out = np.zeros((REACH, 4, 2, 4, GRID), np.float64)
    for k in range(1, REACH + 1):
        for y in range(4):
            out[k - 1, y, 0, y] = cos[:, k]
            out[k - 1, y, 1, y] = -sin[:, k]
    return out.reshape(REACH * 8, 4 * GRID)


def y_spans():
    cols = columns()
    spans = []
    for start in range(0, COLS, TILE):
        ks = [k for _, k in cols[start : start + TILE]]
        spans.append((min(ks) - 1, max(ks)))
    return spans


def y_constant():
    cos, sin = tables()
    cols = columns()
    blocks = []
    for tile, (first, last) in enumerate(y_spans()):
        block = np.zeros((last - first, GRID, 2, 2, TILE), np.float64)
        for lane, (q, k) in enumerate(cols[tile * TILE : (tile + 1) * TILE]):
            block[k - 1 - first, :, 0, 0, lane] = cos[:, q]
            block[k - 1 - first, :, 1, 0, lane] = sin[:, q]
            block[k - 1 - first, :, 0, 1, lane] = -sin[:, q]
            block[k - 1 - first, :, 1, 1, lane] = cos[:, q]
        blocks.append(block.reshape(-1, 2 * TILE))
    return np.concatenate(blocks, 0)


def x_constant():
    cos, sin = tables()
    out = np.zeros((2, PAIR_ROWS, GRID // 2, 2, 2, 2), np.float64)
    for pair in range(2):
        for a in range(-REACH, REACH + 1):
            c = cos[:, a % GRID].reshape(-1, 2)
            s = sin[:, a % GRID].reshape(-1, 2)
            out[pair, a + REACH, :, 0, pair] = c
            out[pair, a + REACH, :, 1, pair] = s
            out[pair, SIDE + a + REACH, :, 0, pair] = -s
            out[pair, SIDE + a + REACH, :, 1, pair] = c
    return out.reshape(2 * PAIR_ROWS, 4 * GRID)


def column_keys():
    keys = np.full((COLS, 1), -1, np.int32)
    for lane, (q, k) in enumerate(columns()):
        keys[lane, 0] = q * GRID + k
    return keys


def transform_kernel(
    row_ref, vi_ref, ci_ref, val_hbm, cond_hbm, zt_hbm, yt_hbm, out_ref,
    val_ref, cond_ref, zt_ref, yt_ref, dens_ref, part_ref, sems,
):
    pairs = dens_ref.shape[0] // 2
    moves = []
    for src, dst, parts in (
        (val_hbm, val_ref, CUTS),
        (cond_hbm, cond_ref, CUTS),
        (zt_hbm, zt_ref, 1),
        (yt_hbm, yt_ref, CUTS),
    ):
        size = src.shape[0] // parts
        for part in range(parts):
            cut = pl.ds(part * size, size)
            moves.append(pltpu.make_async_copy(src.at[cut], dst.at[cut], sems.at[len(moves)]))
            moves[-1].start()
    first_pair = row_ref[0] * pairs
    for move in moves[: 2 * CUTS]:
        move.wait()
    for p in range(pairs):
        dens_ref[2 * p : 2 * p + 2, :] = val_ref[vi_ref[first_pair + p]] * cond_ref[ci_ref[first_pair + p]]
    moves[2 * CUTS].wait()
    for j in range(GRID // 4):
        zt = lax.dot_general(
            zt_ref[...],
            dens_ref[:, j * 256 : (j + 1) * 256],
            (((1,), (1,)), ((), ())),
            preferred_element_type=F32,
        )
        part_ref[:, j * 8 : (j + 1) * 8, :] = zt.reshape(REACH, 8, 2 * pairs)
    low = lax.broadcasted_iota(jnp.int32, (2 * pairs, TILE), 0) % 8 < 4
    for move in moves[2 * CUTS + 1 :]:
        move.wait()
    row = 0
    for tile, (first, last) in enumerate(y_spans()):
        depth = (last - first) * 2 * GRID
        left = part_ref[first:last].astype(BF16).reshape(depth, 2 * pairs)
        both = lax.dot_general(
            left, yt_ref[row : row + depth, :], (((0,), (0,)), ((), ())), preferred_element_type=F32
        )
        row += depth
        real, imag = both[:, :TILE], both[:, TILE:]
        even = jnp.where(low, real, pltpu.roll(imag, 4, 0))
        odd = jnp.where(low, pltpu.roll(real, 2 * pairs - 4, 0), imag)
        for m in range(2 * pairs // 8):
            out_ref[16 * m : 16 * m + 16, tile * TILE : (tile + 1) * TILE] = jnp.concatenate(
                [even[8 * m : 8 * m + 8], odd[8 * m : 8 * m + 8]], 0
            ).astype(BF16)


def transform(row_index, pairs, val_index, cond_index, val_orbitals, cond_orbitals):
    smem = pl.BlockSpec(memory_space=pltpu.SMEM)
    hbm = pl.BlockSpec(memory_space=pltpu.HBM)
    z_table, y_table = z_constant(), y_constant()
    return pl.pallas_call(
        transform_kernel,
        out_shape=jax.ShapeDtypeStruct((4 * pairs, COLS), BF16),
        in_specs=[smem, smem, smem, hbm, hbm, hbm, hbm],
        out_specs=pl.BlockSpec(memory_space=pltpu.VMEM),
        scratch_shapes=[
            pltpu.VMEM(val_orbitals.shape, BF16),
            pltpu.VMEM(cond_orbitals.shape, BF16),
            pltpu.VMEM(z_table.shape, BF16),
            pltpu.VMEM(y_table.shape, BF16),
            pltpu.VMEM((2 * pairs, GRID * GRID), BF16),
            pltpu.VMEM((REACH, 2 * GRID, 2 * pairs), F32),
            pltpu.SemaphoreType.DMA((3 * CUTS + 1,)),
        ],
        compiler_params=pltpu.CompilerParams(vmem_limit_bytes=VMEM_LIMIT),
        name="transform",
    )(
        row_index.reshape(1),
        val_index,
        cond_index,
        val_orbitals,
        cond_orbitals,
        jnp.asarray(z_table, BF16),
        jnp.asarray(y_table, BF16),
    )


def select_kernel(y_ref, xt_ref, key_ref, gmap_ref, out_ref):
    spec = jnp.dot(xt_ref[...], y_ref[...], preferred_element_type=F32)
    spec = (spec * float(GRID) ** (-1.5)).astype(BF16)
    rows, _, width = gmap_ref.shape
    copies = out_ref.shape[0] // rows
    side = lax.broadcasted_iota(jnp.int32, (PAIR_ROWS, width), 0)
    for r in range(rows):
        entry = gmap_ref[r]
        key = entry & (GRID * GRID - 1)
        wave_a = (entry >> 12) & (GRID - 1)
        row = (entry >> 18) * SIDE + ((wave_a + REACH) & (GRID - 1))
        hit = jnp.where(key_ref[...] == key, 1.0, 0.0).astype(BF16)
        found = jnp.dot(spec, hit, preferred_element_type=F32)
        here = side == row
        picked = [
            jnp.sum(jnp.where(here, found[i * PAIR_ROWS : (i + 1) * PAIR_ROWS], 0.0), 0, keepdims=True)
            for i in range(2)
        ]
        both = jnp.concatenate(picked, 0).astype(BF16)
        for copy in range(copies):
            out_ref[r * copies + copy] = both


def select(block, gmap, copies, rows):
    width = NG // rows
    vmem = pl.BlockSpec(memory_space=pltpu.VMEM)
    return pl.pallas_call(
        select_kernel,
        out_shape=jax.ShapeDtypeStruct((rows * copies, 2, width), BF16),
        in_specs=[vmem] * 4,
        out_specs=vmem,
        compiler_params=pltpu.CompilerParams(vmem_limit_bytes=40 * 2**20),
        name="select",
    )(block, jnp.asarray(x_constant(), BF16), jnp.asarray(column_keys()), gmap.reshape(rows, 1, width))


def product_kernel(left_ref, right_ref, weight_ref, out_ref):
    turned = left_ref[...].T.astype(F32)
    for f in range(out_ref.shape[0]):
        weighted = (turned * weight_ref[f : f + 1, :]).astype(BF16)
        part = jnp.dot(weighted, right_ref[...], preferred_element_type=F32)
        out_ref[f] = part * (1.0 / math.sqrt(left_ref.shape[0]))


def product(left, right, weights, step=384):
    pairs, rows = left.shape
    width = right.shape[1]
    return pl.pallas_call(
        product_kernel,
        grid=(rows // step,),
        out_shape=jax.ShapeDtypeStruct((weights.shape[0], rows, width), F32),
        in_specs=[
            pl.BlockSpec((pairs, step), lambda i: (0, i)),
            pl.BlockSpec((pairs, width), lambda i: (0, 0)),
            pl.BlockSpec(weights.shape, lambda i: (0, 0)),
        ],
        out_specs=pl.BlockSpec((weights.shape[0], step, width), lambda i: (0, i, 0)),
        compiler_params=pltpu.CompilerParams(
            dimension_semantics=("arbitrary",), vmem_limit_bytes=32 * 2**20
        ),
        name="product",
    )(left, right, weights)


def pair_weights(val_index, cond_index, val_energy, cond_energy, freqs):
    val_hit = val_index[:, None] == jnp.arange(val_energy.shape[0], dtype=jnp.int32)[None, :]
    cond_hit = cond_index[:, None] == jnp.arange(cond_energy.shape[0], dtype=jnp.int32)[None, :]
    gap = jnp.sum(jnp.where(cond_hit, cond_energy[None, :], 0.0), 1) - jnp.sum(
        jnp.where(val_hit, val_energy[None, :], 0.0), 1
    )
    return -4.0 * gap[None, :] / (gap[None, :] ** 2 + freqs[:, None] ** 2)


ROW = ("x", "z_lo", "core")
COL = ("z_hi", "y")


def reorder(pair_values):
    return pair_values.reshape(16, 4, 8, 2).transpose(2, 0, 1, 3).reshape(-1)


def shards(
    val_orbitals, cond_orbitals, val_index, cond_index, val_energy, cond_energy, freqs, gmap
):
    row_count = lax.axis_size(ROW)
    col_count = lax.axis_size(COL)
    pair_dev = val_index.shape[0] // row_count
    partial = transform(
        lax.axis_index(ROW), pair_dev, val_index, cond_index, val_orbitals, cond_orbitals
    )
    block = lax.all_to_all(
        partial.reshape(col_count, 8, COLS), COL, split_axis=0, concat_axis=0, tiled=True
    ).reshape(4 * GRID, COLS)
    for_rows = select(block, gmap, 4, row_count)
    mine = lax.all_to_all(for_rows, ROW + ("z_hi",), split_axis=0, concat_axis=0, tiled=True)
    wide = NG // row_count
    width = NG // col_count
    z_hi = lax.axis_index("z_hi")
    piece = lax.dynamic_slice(
        mine, (z_hi // 2 * (pair_dev // 2), 0, z_hi % 2 * width), (pair_dev // 2, 2, width)
    )
    column = lax.ppermute(piece, ROW + COL, column_moves())
    copies = jnp.broadcast_to(mine.reshape(1, -1, wide), (lax.axis_size("y"), 2 * mine.shape[0], wide))
    copies, column = lax.optimization_barrier((copies, column))
    left = lax.all_to_all(copies, "y", split_axis=0, concat_axis=0, tiled=True).reshape(-1, wide)
    right = lax.all_gather(column.reshape(pair_dev, width), ROW, axis=0, tiled=True)
    weights = pair_weights(reorder(val_index), reorder(cond_index), val_energy, cond_energy, freqs)
    return product(left, right, weights)


def column_moves():
    moves = []
    for row in range(16):
        for z_hi in range(4):
            for y in range(8):
                moves.append((row * 32 + z_hi * 8 + y, (2 * y + z_hi // 2) * 32 + 2 * row + z_hi % 2))
    return moves


def solution(mesh):
    fine = Mesh(mesh.devices.reshape(4, 2, 2, 4, 8), ROW + COL)
    orbitals = P(None, COL, None)
    placed = (orbitals, orbitals, P(), P(), P(), P(), P(), P())
    return jax.shard_map(
        shards, mesh=fine, in_specs=placed, out_specs=P(None, ROW, COL), check_vma=False
    )
```

```python
import functools
import math

import jax
import jax.numpy as jnp
import numpy as np
from jax import lax
from jax.experimental import pallas as pl
from jax.experimental.pallas import tpu as pltpu
from jax.sharding import Mesh, PartitionSpec as P

GRID = 64
NG = 12288
REACH = 18
SIDE = 2 * REACH + 1
RADIUS2 = 334
COLS = 512
PAIR_ROWS = 80
TILE = 128
CUTS = 1
BF16 = jnp.bfloat16
F32 = jnp.float32
VMEM_LIMIT = 60 * 2**20


def tables():
    idx = np.arange(GRID)
    phase = (idx[:, None] * idx[None, :] % GRID).astype(np.float32) * np.float32(2.0 * math.pi / GRID)
    phase = phase.astype(np.float64)
    return np.cos(phase), np.sin(phase)


def columns():
    found = []
    for k in range(1, REACH + 1):
        for q in range(-REACH, REACH + 1):
            if q * q + k * k <= RADIUS2:
                found.append((q % GRID, k))
    return found


def z_constant():
    cos, sin = tables()
    out = np.zeros((REACH, 4, 2, 4, GRID), np.float64)
    for k in range(1, REACH + 1):
        for y in range(4):
            out[k - 1, y, 0, y] = cos[:, k]
            out[k - 1, y, 1, y] = -sin[:, k]
    return out.reshape(REACH * 8, 4 * GRID)


def y_spans():
    cols = columns()
    spans = []
    for start in range(0, COLS, TILE):
        ks = [k for _, k in cols[start : start + TILE]]
        spans.append((min(ks) - 1, max(ks)))
    return spans


def y_constant():
    cos, sin = tables()
    cols = columns()
    blocks = []
    for tile, (first, last) in enumerate(y_spans()):
        block = np.zeros((last - first, GRID, 2, 2, TILE), np.float64)
        for lane, (q, k) in enumerate(cols[tile * TILE : (tile + 1) * TILE]):
            block[k - 1 - first, :, 0, 0, lane] = cos[:, q]
            block[k - 1 - first, :, 1, 0, lane] = sin[:, q]
            block[k - 1 - first, :, 0, 1, lane] = -sin[:, q]
            block[k - 1 - first, :, 1, 1, lane] = cos[:, q]
        blocks.append(block.reshape(-1, 2 * TILE))
    return np.concatenate(blocks, 0)


def x_constant():
    cos, sin = tables()
    out = np.zeros((2, PAIR_ROWS, GRID // 2, 2, 2, 2), np.float64)
    for pair in range(2):
        for a in range(-REACH, REACH + 1):
            c = cos[:, a % GRID].reshape(-1, 2)
            s = sin[:, a % GRID].reshape(-1, 2)
            out[pair, a + REACH, :, 0, pair] = c
            out[pair, a + REACH, :, 1, pair] = s
            out[pair, SIDE + a + REACH, :, 0, pair] = -s
            out[pair, SIDE + a + REACH, :, 1, pair] = c
    return out.reshape(2 * PAIR_ROWS, 4 * GRID)


def column_keys():
    keys = np.full((COLS, 1), -1, np.int32)
    for lane, (q, k) in enumerate(columns()):
        keys[lane, 0] = q * GRID + k
    return keys


def transform_kernel(
    row_ref, vi_ref, ci_ref, val_hbm, cond_hbm, zt_hbm, yt_hbm, out_ref,
    val_ref, cond_ref, zt_ref, yt_ref, dens_ref, part_ref, sems,
):
    pairs = dens_ref.shape[0] // 2
    moves = []
    for src, dst, parts in (
        (val_hbm, val_ref, CUTS),
        (cond_hbm, cond_ref, CUTS),
        (zt_hbm, zt_ref, 1),
        (yt_hbm, yt_ref, CUTS),
    ):
        size = src.shape[0] // parts
        for part in range(parts):
            cut = pl.ds(part * size, size)
            moves.append(pltpu.make_async_copy(src.at[cut], dst.at[cut], sems.at[len(moves)]))
            moves[-1].start()
    first_pair = row_ref[0] * pairs
    for move in moves[: 2 * CUTS]:
        move.wait()
    for p in range(pairs):
        dens_ref[2 * p : 2 * p + 2, :] = val_ref[vi_ref[first_pair + p]] * cond_ref[ci_ref[first_pair + p]]
    moves[2 * CUTS].wait()
    for j in range(GRID // 4):
        zt = lax.dot_general(
            zt_ref[...],
            dens_ref[:, j * 256 : (j + 1) * 256],
            (((1,), (1,)), ((), ())),
            preferred_element_type=F32,
        )
        part_ref[:, j * 8 : (j + 1) * 8, :] = zt.reshape(REACH, 8, 2 * pairs)
    low = lax.broadcasted_iota(jnp.int32, (2 * pairs, TILE), 0) % 8 < 4
    for move in moves[2 * CUTS + 1 :]:
        move.wait()
    row = 0
    for tile, (first, last) in enumerate(y_spans()):
        depth = (last - first) * 2 * GRID
        left = part_ref[first:last].astype(BF16).reshape(depth, 2 * pairs)
        both = lax.dot_general(
            left, yt_ref[row : row + depth, :], (((0,), (0,)), ((), ())), preferred_element_type=F32
        )
        row += depth
        real, imag = both[:, :TILE], both[:, TILE:]
        even = jnp.where(low, real, pltpu.roll(imag, 4, 0))
        odd = jnp.where(low, pltpu.roll(real, 2 * pairs - 4, 0), imag)
        for m in range(2 * pairs // 8):
            out_ref[16 * m : 16 * m + 16, tile * TILE : (tile + 1) * TILE] = jnp.concatenate(
                [even[8 * m : 8 * m + 8], odd[8 * m : 8 * m + 8]], 0
            ).astype(BF16)


def transform(row_index, pairs, val_index, cond_index, val_orbitals, cond_orbitals):
    smem = pl.BlockSpec(memory_space=pltpu.SMEM)
    hbm = pl.BlockSpec(memory_space=pltpu.HBM)
    z_table, y_table = z_constant(), y_constant()
    return pl.pallas_call(
        transform_kernel,
        out_shape=jax.ShapeDtypeStruct((4 * pairs, COLS), BF16),
        in_specs=[smem, smem, smem, hbm, hbm, hbm, hbm],
        out_specs=pl.BlockSpec(memory_space=pltpu.VMEM),
        scratch_shapes=[
            pltpu.VMEM(val_orbitals.shape, BF16),
            pltpu.VMEM(cond_orbitals.shape, BF16),
            pltpu.VMEM(z_table.shape, BF16),
            pltpu.VMEM(y_table.shape, BF16),
            pltpu.VMEM((2 * pairs, GRID * GRID), BF16),
            pltpu.VMEM((REACH, 2 * GRID, 2 * pairs), F32),
            pltpu.SemaphoreType.DMA((3 * CUTS + 1,)),
        ],
        compiler_params=pltpu.CompilerParams(vmem_limit_bytes=VMEM_LIMIT),
        name="transform",
    )(
        row_index.reshape(1),
        val_index,
        cond_index,
        val_orbitals,
        cond_orbitals,
        jnp.asarray(z_table, BF16),
        jnp.asarray(y_table, BF16),
    )


def select_kernel(y_ref, xt_ref, key_ref, gmap_ref, out_ref):
    spec = jnp.dot(xt_ref[...], y_ref[...], preferred_element_type=F32)
    spec = (spec * float(GRID) ** (-1.5)).astype(BF16)
    rows, _, width = gmap_ref.shape
    copies = out_ref.shape[0] // rows
    side = lax.broadcasted_iota(jnp.int32, (PAIR_ROWS, width), 0)
    for r in range(rows):
        entry = gmap_ref[r]
        key = entry & (GRID * GRID - 1)
        wave_a = (entry >> 12) & (GRID - 1)
        row = (entry >> 18) * SIDE + ((wave_a + REACH) & (GRID - 1))
        hit = jnp.where(key_ref[...] == key, 1.0, 0.0).astype(BF16)
        found = jnp.dot(spec, hit, preferred_element_type=F32)
        here = side == row
        picked = [
            jnp.sum(jnp.where(here, found[i * PAIR_ROWS : (i + 1) * PAIR_ROWS], 0.0), 0, keepdims=True)
            for i in range(2)
        ]
        both = jnp.concatenate(picked, 0).astype(BF16)
        for copy in range(copies):
            out_ref[r * copies + copy] = both


def select(block, gmap, copies, rows):
    width = NG // rows
    vmem = pl.BlockSpec(memory_space=pltpu.VMEM)
    return pl.pallas_call(
        select_kernel,
        out_shape=jax.ShapeDtypeStruct((rows * copies, 2, width), BF16),
        in_specs=[vmem] * 4,
        out_specs=vmem,
        compiler_params=pltpu.CompilerParams(vmem_limit_bytes=40 * 2**20),
        name="select",
    )(block, jnp.asarray(x_constant(), BF16), jnp.asarray(column_keys()), gmap.reshape(rows, 1, width))


def product_kernel(turn_ref, *refs):
    pieces, (right_ref, weight_ref, out_ref, turned_ref) = refs[:-4], refs[-4:]
    pairs = right_ref.shape[0]
    part = pairs // len(pieces)
    for shift, piece in enumerate(pieces):
        place = lax.rem(turn_ref[0] + shift, len(pieces))
        turned_ref[:, pl.ds(pl.multiple_of(place * part, part), part)] = piece[...].T
    turned = turned_ref[...].astype(F32)
    for f in range(out_ref.shape[0]):
        weighted = (turned * weight_ref[f : f + 1, :]).astype(BF16)
        total = jnp.dot(weighted, right_ref[...], preferred_element_type=F32)
        out_ref[f] = total * (1.0 / math.sqrt(pairs))


def product(turn, pieces, right, weights, step=384):
    part, rows = pieces[0].shape
    pairs, width = right.shape
    return pl.pallas_call(
        product_kernel,
        grid=(rows // step,),
        out_shape=jax.ShapeDtypeStruct((weights.shape[0], rows, width), F32),
        in_specs=[pl.BlockSpec(memory_space=pltpu.SMEM)]
        + [pl.BlockSpec((part, step), lambda i: (0, i)) for _ in pieces]
        + [
            pl.BlockSpec((pairs, width), lambda i: (0, 0)),
            pl.BlockSpec(weights.shape, lambda i: (0, 0)),
        ],
        out_specs=pl.BlockSpec((weights.shape[0], step, width), lambda i: (0, i, 0)),
        scratch_shapes=[pltpu.VMEM((step, pairs), BF16)],
        compiler_params=pltpu.CompilerParams(
            dimension_semantics=("arbitrary",), vmem_limit_bytes=32 * 2**20
        ),
        name="product",
    )(turn.reshape(1), *pieces, right, weights)


def pair_weights(val_index, cond_index, val_energy, cond_energy, freqs):
    val_hit = val_index[:, None] == jnp.arange(val_energy.shape[0], dtype=jnp.int32)[None, :]
    cond_hit = cond_index[:, None] == jnp.arange(cond_energy.shape[0], dtype=jnp.int32)[None, :]
    gap = jnp.sum(jnp.where(cond_hit, cond_energy[None, :], 0.0), 1) - jnp.sum(
        jnp.where(val_hit, val_energy[None, :], 0.0), 1
    )
    return -4.0 * gap[None, :] / (gap[None, :] ** 2 + freqs[:, None] ** 2)


ROW = ("x", "z_lo", "core")
COL = ("z_hi", "y")


def reorder(pair_values):
    return pair_values.reshape(16, 4, 8, 2).transpose(2, 0, 1, 3).reshape(-1)


def shards(
    val_orbitals, cond_orbitals, val_index, cond_index, val_energy, cond_energy, freqs, gmap
):
    row_count = lax.axis_size(ROW)
    col_count = lax.axis_size(COL)
    pair_dev = val_index.shape[0] // row_count
    partial = transform(
        lax.axis_index(ROW), pair_dev, val_index, cond_index, val_orbitals, cond_orbitals
    )
    block = lax.all_to_all(
        partial.reshape(col_count, 8, COLS), COL, split_axis=0, concat_axis=0, tiled=True
    ).reshape(4 * GRID, COLS)
    for_rows = select(block, gmap, 4, row_count)
    mine = lax.all_to_all(for_rows, ROW + ("z_hi",), split_axis=0, concat_axis=0, tiled=True)
    wide = NG // row_count
    width = NG // col_count
    z_hi = lax.axis_index("z_hi")
    piece = lax.dynamic_slice(
        mine, (z_hi // 2 * (pair_dev // 2), 0, z_hi % 2 * width), (pair_dev // 2, 2, width)
    )
    column = lax.ppermute(piece, ROW + COL, column_moves())
    pieces = gather_y(mine.reshape(-1, wide))
    right = lax.all_to_all(
        jnp.broadcast_to(column.reshape(pair_dev, width), (row_count, pair_dev, width)),
        ROW, split_axis=0, concat_axis=0, tiled=True,
    ).reshape(-1, width)
    weights = pair_weights(reorder(val_index), reorder(cond_index), val_energy, cond_energy, freqs)
    return product(lax.axis_index("y"), pieces, right, weights)


def gather_y(block):
    count = lax.axis_size("y")

    def fetch(value, ahead):
        return lax.ppermute(value, "y", [((i + ahead) % count, i) for i in range(count)])

    one, last = fetch(block, 1), fetch(block, -1)
    two, back_two = fetch(block, 2), fetch(block, -2)
    three, back_three = fetch(two, 1), fetch(back_two, -1)
    four = fetch(two, 2)
    return [block, one, two, three, four, back_three, back_two, last]


def column_moves():
    moves = []
    for row in range(16):
        for z_hi in range(4):
            for y in range(8):
                moves.append((row * 32 + z_hi * 8 + y, (2 * y + z_hi // 2) * 32 + 2 * row + z_hi % 2))
    return moves


def solution(mesh):
    fine = Mesh(mesh.devices.reshape(4, 2, 2, 4, 8), ROW + COL)
    orbitals = P(None, COL, None)
    placed = (orbitals, orbitals, P(), P(), P(), P(), P(), P())
    return jax.shard_map(
        shards, mesh=fine, in_specs=placed, out_specs=P(None, ROW, COL), check_vma=False
    )
```

```python
import functools
import math

import jax
import jax.numpy as jnp
import numpy as np
from jax import lax
from jax.experimental import pallas as pl
from jax.experimental.pallas import tpu as pltpu
from jax.sharding import Mesh, PartitionSpec as P

GRID = 64
NG = 12288
REACH = 18
SIDE = 2 * REACH + 1
RADIUS2 = 334
COLS = 512
PAIR_ROWS = 80
TILE = 128
BF16 = jnp.bfloat16
F32 = jnp.float32
VMEM_LIMIT = 60 * 2**20


def tables():
    idx = np.arange(GRID)
    phase = (idx[:, None] * idx[None, :] % GRID).astype(np.float32) * np.float32(2.0 * math.pi / GRID)
    phase = phase.astype(np.float64)
    return np.cos(phase), np.sin(phase)


def columns():
    found = []
    for k in range(1, REACH + 1):
        for q in range(-REACH, REACH + 1):
            if q * q + k * k <= RADIUS2:
                found.append((q % GRID, k))
    return found


def z_constant():
    cos, sin = tables()
    out = np.zeros((REACH, 4, 2, 4, GRID), np.float64)
    for k in range(1, REACH + 1):
        for y in range(4):
            out[k - 1, y, 0, y] = cos[:, k]
            out[k - 1, y, 1, y] = -sin[:, k]
    return out.reshape(REACH * 8, 4 * GRID)


def y_spans():
    cols = columns()
    spans = []
    for start in range(0, COLS, TILE):
        ks = [k for _, k in cols[start : start + TILE]]
        spans.append((min(ks) - 1, max(ks)))
    return spans


def y_constant():
    cos, sin = tables()
    out = np.zeros((2, GRID, 2, TILE), np.float64)
    for q in range(-REACH, REACH + 1):
        out[0, :, 0, q + REACH] = cos[:, q % GRID]
        out[0, :, 1, q + REACH] = sin[:, q % GRID]
        out[1, :, 0, q + REACH] = -sin[:, q % GRID]
        out[1, :, 1, q + REACH] = cos[:, q % GRID]
    return out.reshape(2, 2 * GRID, TILE)


def y_runs():
    cols = columns()
    runs = []
    for tile, (first, last) in enumerate(y_spans()):
        own = cols[tile * TILE : (tile + 1) * TILE]
        for k in range(first + 1, last + 1):
            lanes = [lane for lane, col in enumerate(own) if col[1] == k]
            q = own[lanes[0]][0]
            runs.append((lanes[0], lanes[-1] + 1, (q + REACH) % GRID))
    return runs


def x_constant():
    cos, sin = tables()
    out = np.zeros((2, PAIR_ROWS, GRID // 2, 2, 2, 2), np.float64)
    for pair in range(2):
        for a in range(-REACH, REACH + 1):
            c = cos[:, a % GRID].reshape(-1, 2)
            s = sin[:, a % GRID].reshape(-1, 2)
            out[pair, a + REACH, :, 0, pair] = c
            out[pair, a + REACH, :, 1, pair] = s
            out[pair, SIDE + a + REACH, :, 0, pair] = -s
            out[pair, SIDE + a + REACH, :, 1, pair] = c
    return out.reshape(2 * PAIR_ROWS, 4 * GRID)


def column_keys():
    keys = np.full((COLS, 1), -1, np.int32)
    for lane, (q, k) in enumerate(columns()):
        keys[lane, 0] = q * GRID + k
    return keys


def transform_kernel(
    val_hbm, cond_hbm, vi_hbm, ci_hbm, yq_hbm, zt_hbm, out_ref,
    val_ref, cond_ref, vi_ref, ci_ref, yq_ref, zt_ref, yt_ref, dens_ref, part_ref, sems,
):
    pairs = dens_ref.shape[0] // 2
    moves = [
        pltpu.make_async_copy(src, dst, sems.at[i])
        for i, (src, dst) in enumerate(
            (
                (yq_hbm, yq_ref),
                (val_hbm, val_ref),
                (cond_hbm, cond_ref),
                (vi_hbm, vi_ref),
                (ci_hbm, ci_ref),
                (zt_hbm, zt_ref),
            )
        )
    ]
    for move in moves:
        move.start()
    moves[0].wait()
    lane = lax.broadcasted_iota(jnp.int32, (2 * GRID, TILE), 1)
    for i, (first, last, place) in enumerate(y_runs()):
        inside = (lane >= first) & (lane < last)
        for out in range(2):
            moved = pltpu.roll(yq_ref[out], (first - place) % TILE, 1)
            yt_ref[2 * GRID * i : 2 * GRID * (i + 1), out * TILE : (out + 1) * TILE] = jnp.where(
                inside, moved, 0.0
            ).astype(BF16)
    first_pair = (
        (lax.axis_index("x") * 2 + lax.axis_index("z_lo")) * 2 + lax.axis_index("core")
    ) * pairs
    for move in moves[1:]:
        move.wait()
    for p in range(pairs):
        val = val_ref[vi_ref[first_pair + p]]
        cond = cond_ref[ci_ref[first_pair + p]]
        dens_ref[2 * p : 2 * p + 2, :] = val * cond
    for j in range(GRID // 4):
        zt = lax.dot_general(
            zt_ref[...],
            dens_ref[:, j * 256 : (j + 1) * 256],
            (((1,), (1,)), ((), ())),
            preferred_element_type=F32,
        )
        part_ref[:, j * 8 : (j + 1) * 8, :] = zt.reshape(REACH, 8, 2 * pairs)
    low = lax.broadcasted_iota(jnp.int32, (2 * pairs, TILE), 0) % 8 < 4
    row = 0
    for tile, (first, last) in enumerate(y_spans()):
        depth = (last - first) * 2 * GRID
        left = part_ref[first:last].astype(BF16).reshape(depth, 2 * pairs)
        both = lax.dot_general(
            left, yt_ref[row : row + depth, :], (((0,), (0,)), ((), ())), preferred_element_type=F32
        )
        row += depth
        real, imag = both[:, :TILE], both[:, TILE:]
        even = jnp.where(low, real, pltpu.roll(imag, 4, 0))
        odd = jnp.where(low, pltpu.roll(real, 2 * pairs - 4, 0), imag)
        for m in range(2 * pairs // 8):
            out_ref[16 * m : 16 * m + 16, tile * TILE : (tile + 1) * TILE] = jnp.concatenate(
                [even[8 * m : 8 * m + 8], odd[8 * m : 8 * m + 8]], 0
            ).astype(BF16)


def transform(pairs, val_index, cond_index, val_orbitals, cond_orbitals):
    hbm = pl.BlockSpec(memory_space=pltpu.HBM)
    y_table = jnp.asarray(jnp.asarray(y_constant(), BF16), F32)
    z_table = jnp.asarray(z_constant(), BF16)
    return pl.pallas_call(
        transform_kernel,
        out_shape=jax.ShapeDtypeStruct((4 * pairs, COLS), BF16),
        in_specs=[hbm] * 6,
        out_specs=pl.BlockSpec(memory_space=pltpu.VMEM),
        scratch_shapes=[
            pltpu.VMEM(val_orbitals.shape, BF16),
            pltpu.VMEM(cond_orbitals.shape, BF16),
            pltpu.SMEM(val_index.shape, jnp.int32),
            pltpu.SMEM(cond_index.shape, jnp.int32),
            pltpu.VMEM(y_table.shape, F32),
            pltpu.VMEM(z_table.shape, BF16),
            pltpu.VMEM((len(y_runs()) * 2 * GRID, 2 * TILE), BF16),
            pltpu.VMEM((2 * pairs, GRID * GRID), BF16),
            pltpu.VMEM((REACH, 2 * GRID, 2 * pairs), F32),
            pltpu.SemaphoreType.DMA((6,)),
        ],
        compiler_params=pltpu.CompilerParams(vmem_limit_bytes=VMEM_LIMIT),
        name="transform",
    )(val_orbitals, cond_orbitals, val_index, cond_index, y_table, z_table)


def select_kernel(y_ref, xt_ref, key_ref, gmap_ref, out_ref):
    spec = jnp.dot(xt_ref[...], y_ref[...], preferred_element_type=F32)
    spec = (spec * float(GRID) ** (-1.5)).astype(BF16)
    rows, _, width = gmap_ref.shape
    copies = out_ref.shape[0] // rows
    side = lax.broadcasted_iota(jnp.int32, (PAIR_ROWS, width), 0)
    for r in range(rows):
        entry = gmap_ref[r]
        key = entry & (GRID * GRID - 1)
        wave_a = (entry >> 12) & (GRID - 1)
        row = (entry >> 18) * SIDE + ((wave_a + REACH) & (GRID - 1))
        hit = jnp.where(key_ref[...] == key, 1.0, 0.0).astype(BF16)
        found = jnp.dot(spec, hit, preferred_element_type=F32)
        here = side == row
        picked = [
            jnp.sum(jnp.where(here, found[i * PAIR_ROWS : (i + 1) * PAIR_ROWS], 0.0), 0, keepdims=True)
            for i in range(2)
        ]
        both = jnp.concatenate(picked, 0).astype(BF16)
        for copy in range(copies):
            out_ref[r * copies + copy] = both


def select(block, gmap, copies, rows):
    width = NG // rows
    vmem = pl.BlockSpec(memory_space=pltpu.VMEM)
    return pl.pallas_call(
        select_kernel,
        out_shape=jax.ShapeDtypeStruct((rows * copies, 2, width), BF16),
        in_specs=[vmem] * 4,
        out_specs=vmem,
        compiler_params=pltpu.CompilerParams(vmem_limit_bytes=40 * 2**20),
        name="select",
    )(block, jnp.asarray(x_constant(), BF16), jnp.asarray(column_keys()), gmap.reshape(rows, 1, width))


def product_kernel(left_ref, right_ref, weight_ref, out_ref):
    turned = left_ref[...].T.astype(F32)
    for f in range(out_ref.shape[0]):
        weighted = (turned * weight_ref[f : f + 1, :]).astype(BF16)
        part = jnp.dot(weighted, right_ref[...], preferred_element_type=F32)
        out_ref[f] = part * (1.0 / math.sqrt(left_ref.shape[0]))


def product(left, right, weights, step=384):
    pairs, rows = left.shape
    width = right.shape[1]
    return pl.pallas_call(
        product_kernel,
        grid=(rows // step,),
        out_shape=jax.ShapeDtypeStruct((weights.shape[0], rows, width), F32),
        in_specs=[
            pl.BlockSpec((pairs, step), lambda i: (0, i)),
            pl.BlockSpec((pairs, width), lambda i: (0, 0)),
            pl.BlockSpec(weights.shape, lambda i: (0, 0)),
        ],
        out_specs=pl.BlockSpec((weights.shape[0], step, width), lambda i: (0, i, 0)),
        compiler_params=pltpu.CompilerParams(
            dimension_semantics=("arbitrary",), vmem_limit_bytes=VMEM_LIMIT
        ),
        name="product",
    )(left, right, weights)


def pair_weights(val_index, cond_index, val_energy, cond_energy, freqs):
    val_hit = val_index[:, None] == jnp.arange(val_energy.shape[0], dtype=jnp.int32)[None, :]
    cond_hit = cond_index[:, None] == jnp.arange(cond_energy.shape[0], dtype=jnp.int32)[None, :]
    gap = jnp.sum(jnp.where(cond_hit, cond_energy[None, :], 0.0), 1) - jnp.sum(
        jnp.where(val_hit, val_energy[None, :], 0.0), 1
    )
    return -4.0 * gap[None, :] / (gap[None, :] ** 2 + freqs[:, None] ** 2)


ROW = ("x", "z_lo", "core")
COL = ("z_hi", "y")


def reorder(pair_values):
    return pair_values.reshape(16, 4, 8, 2).transpose(2, 0, 1, 3).reshape(-1)


def shards(
    val_orbitals, cond_orbitals, val_index, cond_index, val_energy, cond_energy, freqs, gmap
):
    row_count = lax.axis_size(ROW)
    col_count = lax.axis_size(COL)
    pair_dev = val_index.shape[0] // row_count
    partial = transform(pair_dev, val_index, cond_index, val_orbitals, cond_orbitals)
    block = lax.all_to_all(
        partial.reshape(col_count, 8, COLS), COL, split_axis=0, concat_axis=0, tiled=True
    ).reshape(4 * GRID, COLS)
    for_rows = select(block, gmap, 4, row_count)
    mine = lax.all_to_all(for_rows, ROW + ("z_hi",), split_axis=0, concat_axis=0, tiled=True)
    mine = mine.reshape(-1, NG // row_count)
    left = lax.all_gather(mine, "y", axis=0, tiled=True)
    width = NG // col_count
    z_hi = lax.axis_index("z_hi")
    piece = lax.dynamic_slice(mine, (z_hi // 2 * pair_dev, z_hi % 2 * width), (pair_dev, width))
    column = lax.ppermute(piece, ROW + COL, column_moves())
    right = lax.all_to_all(
        jnp.broadcast_to(column, (row_count, pair_dev, width)), ROW, split_axis=0, concat_axis=0, tiled=True
    ).reshape(-1, width)
    weights = pair_weights(reorder(val_index), reorder(cond_index), val_energy, cond_energy, freqs)
    return product(left, right, weights)


def column_moves():
    moves = []
    for row in range(16):
        for z_hi in range(4):
            for y in range(8):
                moves.append((row * 32 + z_hi * 8 + y, (2 * y + z_hi // 2) * 32 + 2 * row + z_hi % 2))
    return moves


def solution(mesh):
    fine = Mesh(mesh.devices.reshape(4, 2, 2, 4, 8), ROW + COL)
    orbitals = P(None, COL, None)
    placed = (orbitals, orbitals, P(), P(), P(), P(), P(), P())
    return jax.shard_map(
        shards, mesh=fine, in_specs=placed, out_specs=P(None, ROW, COL), check_vma=False
    )
```

```python
import functools
import math

import jax
import jax.numpy as jnp
import numpy as np
from jax import lax
from jax.experimental import pallas as pl
from jax.experimental.pallas import tpu as pltpu
from jax.sharding import Mesh, PartitionSpec as P

GRID = 64
NG = 12288
PAIRS = 1024
REACH = 18
SIDE = 2 * REACH + 1
RADIUS2 = 334
COLS = 512
PAIR_ROWS = 80
TILE = 128
BF16 = jnp.bfloat16
F32 = jnp.float32
VMEM_LIMIT = 60 * 2**20


def tables():
    idx = np.arange(GRID)
    phase = (idx[:, None] * idx[None, :] % GRID).astype(np.float32) * np.float32(2.0 * math.pi / GRID)
    phase = phase.astype(np.float64)
    return np.cos(phase), np.sin(phase)


def columns():
    found = []
    for k in range(1, REACH + 1):
        for q in range(-REACH, REACH + 1):
            if q * q + k * k <= RADIUS2:
                found.append((q % GRID, k))
    return found


def z_constant():
    cos, sin = tables()
    out = np.zeros((REACH, 4, 2, 4, GRID), np.float64)
    for k in range(1, REACH + 1):
        for y in range(4):
            out[k - 1, y, 0, y] = cos[:, k]
            out[k - 1, y, 1, y] = -sin[:, k]
    return out.reshape(REACH * 8, 4 * GRID)


def y_spans():
    cols = columns()
    spans = []
    for start in range(0, COLS, TILE):
        ks = [k for _, k in cols[start : start + TILE]]
        spans.append((min(ks) - 1, max(ks)))
    return spans


def y_constant():
    cos, sin = tables()
    out = np.zeros((2, GRID, 2, TILE), np.float64)
    for q in range(-REACH, REACH + 1):
        out[0, :, 0, q + REACH] = cos[:, q % GRID]
        out[0, :, 1, q + REACH] = sin[:, q % GRID]
        out[1, :, 0, q + REACH] = -sin[:, q % GRID]
        out[1, :, 1, q + REACH] = cos[:, q % GRID]
    return out.reshape(2, 2 * GRID, TILE)


def y_runs():
    cols = columns()
    runs = []
    for tile, (first, last) in enumerate(y_spans()):
        own = cols[tile * TILE : (tile + 1) * TILE]
        for k in range(first + 1, last + 1):
            lanes = [lane for lane, col in enumerate(own) if col[1] == k]
            q = own[lanes[0]][0]
            runs.append((lanes[0], lanes[-1] + 1, (q + REACH) % GRID))
    return runs


def x_constant():
    cos, sin = tables()
    out = np.zeros((2, PAIR_ROWS, GRID // 2, 2, 2, 2), np.float64)
    for pair in range(2):
        for a in range(-REACH, REACH + 1):
            c = cos[:, a % GRID].reshape(-1, 2)
            s = sin[:, a % GRID].reshape(-1, 2)
            out[pair, a + REACH, :, 0, pair] = c
            out[pair, a + REACH, :, 1, pair] = s
            out[pair, SIDE + a + REACH, :, 0, pair] = -s
            out[pair, SIDE + a + REACH, :, 1, pair] = c
    return out.reshape(2 * PAIR_ROWS, 4 * GRID)


def column_keys():
    keys = np.full((COLS, 1), -1, np.int32)
    for lane, (q, k) in enumerate(columns()):
        keys[lane, 0] = q * GRID + k
    return keys


def transform_kernel(
    val_hbm, cond_hbm, vi_hbm, ci_hbm, yq_hbm, zt_hbm, out_ref,
    val_ref, cond_ref, vi_ref, ci_ref, yq_ref, zt_ref, yt_ref, dens_ref, part_ref, sems,
):
    pairs = dens_ref.shape[0] // 2
    moves = [
        pltpu.make_async_copy(src, dst, sems.at[i])
        for i, (src, dst) in enumerate(
            (
                (yq_hbm, yq_ref),
                (val_hbm, val_ref),
                (cond_hbm, cond_ref),
                (vi_hbm, vi_ref),
                (ci_hbm, ci_ref),
                (zt_hbm, zt_ref),
            )
        )
    ]
    for move in moves:
        move.start()
    moves[0].wait()
    lane = lax.broadcasted_iota(jnp.int32, (2 * GRID, TILE), 1)
    for i, (first, last, place) in enumerate(y_runs()):
        inside = (lane >= first) & (lane < last)
        for out in range(2):
            moved = pltpu.roll(yq_ref[out], (first - place) % TILE, 1)
            yt_ref[2 * GRID * i : 2 * GRID * (i + 1), out * TILE : (out + 1) * TILE] = jnp.where(
                inside, moved, 0.0
            ).astype(BF16)
    first_pair = (
        (lax.axis_index("x") * 2 + lax.axis_index("z_lo")) * 2 + lax.axis_index("core")
    ) * pairs
    for move in moves[1:]:
        move.wait()
    for p in range(pairs):
        val = val_ref[vi_ref[first_pair + p]]
        cond = cond_ref[ci_ref[first_pair + p]]
        dens_ref[2 * p : 2 * p + 2, :] = val * cond
    for j in range(GRID // 4):
        zt = lax.dot_general(
            zt_ref[...],
            dens_ref[:, j * 256 : (j + 1) * 256],
            (((1,), (1,)), ((), ())),
            preferred_element_type=F32,
        )
        part_ref[:, j * 8 : (j + 1) * 8, :] = zt.reshape(REACH, 8, 2 * pairs)
    low = lax.broadcasted_iota(jnp.int32, (2 * pairs, TILE), 0) % 8 < 4
    row = 0
    for tile, (first, last) in enumerate(y_spans()):
        depth = (last - first) * 2 * GRID
        left = part_ref[first:last].astype(BF16).reshape(depth, 2 * pairs)
        both = lax.dot_general(
            left, yt_ref[row : row + depth, :], (((0,), (0,)), ((), ())), preferred_element_type=F32
        )
        row += depth
        real, imag = both[:, :TILE], both[:, TILE:]
        even = jnp.where(low, real, pltpu.roll(imag, 4, 0))
        odd = jnp.where(low, pltpu.roll(real, 2 * pairs - 4, 0), imag)
        for m in range(2 * pairs // 8):
            out_ref[16 * m : 16 * m + 16, tile * TILE : (tile + 1) * TILE] = jnp.concatenate(
                [even[8 * m : 8 * m + 8], odd[8 * m : 8 * m + 8]], 0
            ).astype(BF16)


def transform(pairs, val_index, cond_index, val_orbitals, cond_orbitals):
    hbm = pl.BlockSpec(memory_space=pltpu.HBM)
    y_table = jnp.asarray(jnp.asarray(y_constant(), BF16), F32)
    z_table = jnp.asarray(z_constant(), BF16)
    return pl.pallas_call(
        transform_kernel,
        out_shape=jax.ShapeDtypeStruct((4 * pairs, COLS), BF16),
        in_specs=[hbm] * 6,
        out_specs=pl.BlockSpec(memory_space=pltpu.VMEM),
        scratch_shapes=[
            pltpu.VMEM(val_orbitals.shape, BF16),
            pltpu.VMEM(cond_orbitals.shape, BF16),
            pltpu.SMEM(val_index.shape, jnp.int32),
            pltpu.SMEM(cond_index.shape, jnp.int32),
            pltpu.VMEM(y_table.shape, F32),
            pltpu.VMEM(z_table.shape, BF16),
            pltpu.VMEM((len(y_runs()) * 2 * GRID, 2 * TILE), BF16),
            pltpu.VMEM((2 * pairs, GRID * GRID), BF16),
            pltpu.VMEM((REACH, 2 * GRID, 2 * pairs), F32),
            pltpu.SemaphoreType.DMA((6,)),
        ],
        compiler_params=pltpu.CompilerParams(vmem_limit_bytes=VMEM_LIMIT),
        name="transform",
    )(val_orbitals, cond_orbitals, val_index, cond_index, y_table, z_table)


def select_kernel(y_ref, xt_ref, key_ref, gmap_ref, out_ref):
    spec = jnp.dot(xt_ref[...], y_ref[...], preferred_element_type=F32)
    spec = (spec * float(GRID) ** (-1.5)).astype(BF16)
    rows, _, width = gmap_ref.shape
    half = width // 2
    side = lax.broadcasted_iota(jnp.int32, (PAIR_ROWS, width), 0)
    for r in range(rows):
        entry = gmap_ref[r]
        key = entry & (GRID * GRID - 1)
        wave_a = (entry >> 12) & (GRID - 1)
        row = (entry >> 18) * SIDE + ((wave_a + REACH) & (GRID - 1))
        hit = jnp.where(key_ref[...] == key, 1.0, 0.0).astype(BF16)
        found = jnp.dot(spec, hit, preferred_element_type=F32)
        here = side == row
        picked = [
            jnp.sum(jnp.where(here, found[i * PAIR_ROWS : (i + 1) * PAIR_ROWS], 0.0), 0, keepdims=True)
            for i in range(2)
        ]
        both = jnp.concatenate(picked, 0).astype(BF16)
        halves = both[:, :half], both[:, half:]
        for col in range(2 * rows):
            out_ref[r * 2 * rows + col, :, :half] = halves[col % 2]
        for which in range(2):
            col = 2 * r + which
            for other in range(rows):
                start = other % 2 * TILE
                out_ref[other * 2 * rows + col, :, half:] = halves[which][:, start : start + 2 * TILE]


def select(block, gmap, rows):
    width = NG // rows
    vmem = pl.BlockSpec(memory_space=pltpu.VMEM)
    return pl.pallas_call(
        select_kernel,
        out_shape=jax.ShapeDtypeStruct((2 * rows * rows, 2, width // 2 + 2 * TILE), BF16),
        in_specs=[vmem] * 4,
        out_specs=vmem,
        compiler_params=pltpu.CompilerParams(vmem_limit_bytes=32 * 2**20),
        name="select",
    )(block, jnp.asarray(x_constant(), BF16), jnp.asarray(column_keys()), gmap.reshape(rows, 1, width))


def half_product(left, right, weight_ref, out_ref, res_ref, sems, half):
    pairs, rows = left.shape
    turned = left.T.astype(F32)
    place = pl.ds(pl.multiple_of(half * rows, rows), rows)
    moves = []
    for f in range(weight_ref.shape[0]):
        weighted = (turned * weight_ref[f : f + 1, :]).astype(BF16)
        total = jnp.dot(weighted, right, preferred_element_type=F32)
        res_ref[f] = total * (1.0 / math.sqrt(pairs))
        moves.append(pltpu.make_async_copy(res_ref.at[f], out_ref.at[f, place], sems.at[f]))
        moves[-1].start()
    for move in moves:
        move.wait()


def own_kernel(mine_ref, third_ref, weight_ref, out_ref, right_ref, res_ref, sems):
    pairs = right_ref.shape[0]
    half = mine_ref.shape[2] - 2 * TILE
    core = lax.axis_index("core")
    here = pl.ds(pl.multiple_of(core * TILE, TILE), 2 * TILE)
    there = pl.ds(pl.multiple_of((1 - core) * 2 * TILE, TILE), TILE)
    right_ref[:, here] = mine_ref[:, :, half:].reshape(pairs, 2 * TILE)
    right_ref[:, there] = third_ref[...].reshape(pairs, TILE)
    left = mine_ref[:, :, :half].reshape(pairs, half)
    half_product(left, right_ref[...], weight_ref, out_ref, res_ref, sems, lax.axis_index("y") % 2)


def rest_kernel(low_ref, high_ref, right_ref, weight_ref, begun_ref, out_ref, res_ref, sems):
    part, _, half = low_ref.shape
    left = jnp.concatenate(
        [low_ref[...].reshape(2 * part, half), high_ref[...].reshape(2 * part, half)], 0
    )
    half_product(left, right_ref[...], weight_ref, out_ref, res_ref, sems, 1 - lax.axis_index("y") % 2)


def half_call(kernel, name, in_specs, out_shape, out_specs, half, width, aliases):
    work = 2 * 2 * PAIRS * half * width
    return pl.pallas_call(
        kernel,
        out_shape=out_shape,
        in_specs=in_specs,
        out_specs=out_specs,
        scratch_shapes=[pltpu.VMEM((2, half, width), F32), pltpu.SemaphoreType.DMA((2,))],
        input_output_aliases=aliases,
        cost_estimate=pl.CostEstimate(flops=work, bytes_accessed=5 * 2**20, transcendentals=0),
        compiler_params=pltpu.CompilerParams(vmem_limit_bytes=32 * 2**20),
        name=name,
    )


def own_product(mine, third, weights, rows, width):
    vmem = pl.BlockSpec(memory_space=pltpu.VMEM)
    hbm = pl.BlockSpec(memory_space=pltpu.HBM)
    shapes = (
        jax.ShapeDtypeStruct((weights.shape[0], rows, width), F32),
        jax.ShapeDtypeStruct((PAIRS, width), BF16),
    )
    call = half_call(own_kernel, "own_half", [vmem] * 3, shapes, (hbm, vmem), rows // 2, width, {})
    return call(mine, third, weights)


def rest_product(low, high, right, weights, begun):
    vmem = pl.BlockSpec(memory_space=pltpu.VMEM)
    hbm = pl.BlockSpec(memory_space=pltpu.HBM)
    _, rows, width = begun.shape
    shape = jax.ShapeDtypeStruct(begun.shape, F32)
    specs = [vmem] * 4 + [hbm]
    call = half_call(rest_kernel, "other_half", specs, shape, hbm, rows // 2, width, {4: 0})
    return call(low, high, right, weights, begun)


def pair_weights(val_index, cond_index, val_energy, cond_energy, freqs):
    val_hit = val_index[:, None] == jnp.arange(val_energy.shape[0], dtype=jnp.int32)[None, :]
    cond_hit = cond_index[:, None] == jnp.arange(cond_energy.shape[0], dtype=jnp.int32)[None, :]
    gap = jnp.sum(jnp.where(cond_hit, cond_energy[None, :], 0.0), 1) - jnp.sum(
        jnp.where(val_hit, val_energy[None, :], 0.0), 1
    )
    return -4.0 * gap[None, :] / (gap[None, :] ** 2 + freqs[:, None] ** 2)


ROW = ("x", "z_lo", "core")
COL = ("z_hi", "y")


def shards(
    val_orbitals, cond_orbitals, val_index, cond_index, val_energy, cond_energy, freqs, gmap
):
    row_count = lax.axis_size(ROW)
    col_count = lax.axis_size(COL)
    pair_dev = val_index.shape[0] // row_count
    partial = transform(pair_dev, val_index, cond_index, val_orbitals, cond_orbitals)
    block = lax.all_to_all(
        partial.reshape(col_count, 8, COLS), COL, split_axis=0, concat_axis=0, tiled=True
    ).reshape(4 * GRID, COLS)
    mine = lax.all_to_all(
        select(block, gmap, row_count), ROW + COL, split_axis=0, concat_axis=0, tiled=True
    )
    sources = mine.shape[0] // 2
    rows, width = NG // row_count, NG // col_count
    half = rows // 2
    third = lax.dynamic_slice(
        mine, (0, 0, half + lax.axis_index("core") * TILE), (2 * sources, 2, TILE)
    )
    third = lax.ppermute(third, "core", [(0, 1), (1, 0)])
    count = lax.axis_size("y")
    low = lax.ppermute(mine[:sources, :, :half], "y", [((i + 1) % count, i) for i in range(count)])
    high = lax.ppermute(mine[sources:, :, :half], "y", [(i, (i + 1) % count) for i in range(count)])
    weights = pair_weights(val_index, cond_index, val_energy, cond_energy, freqs)
    begun, right = own_product(mine, third, weights, rows, width)
    return rest_product(low, high, right, weights, begun)


def solution(mesh):
    fine = Mesh(mesh.devices.reshape(4, 2, 2, 4, 8), ROW + COL)
    orbitals = P(None, COL, None)
    placed = (orbitals, orbitals, P(), P(), P(), P(), P(), P())
    return jax.shard_map(
        shards, mesh=fine, in_specs=placed, out_specs=P(None, ROW, COL), check_vma=False
    )
```

```python
import functools
import math

import jax
import jax.numpy as jnp
import numpy as np
from jax import lax
from jax.experimental import pallas as pl
from jax.experimental.pallas import tpu as pltpu
from jax.sharding import Mesh, PartitionSpec as P

GRID = 64
NG = 12288
PAIRS = 1024
REACH = 18
SIDE = 2 * REACH + 1
RADIUS2 = 334
COLS = 512
PAIR_ROWS = 80
TILE = 128
BF16 = jnp.bfloat16
F32 = jnp.float32
VMEM_LIMIT = 60 * 2**20


def tables():
    idx = np.arange(GRID)
    phase = (idx[:, None] * idx[None, :] % GRID).astype(np.float32) * np.float32(2.0 * math.pi / GRID)
    phase = phase.astype(np.float64)
    return np.cos(phase), np.sin(phase)


def columns():
    found = []
    for k in range(1, REACH + 1):
        for q in range(-REACH, REACH + 1):
            if q * q + k * k <= RADIUS2:
                found.append((q % GRID, k))
    return found


def z_constant():
    cos, sin = tables()
    out = np.zeros((REACH, 4, 2, 4, GRID), np.float64)
    for k in range(1, REACH + 1):
        for y in range(4):
            out[k - 1, y, 0, y] = cos[:, k]
            out[k - 1, y, 1, y] = -sin[:, k]
    return out.reshape(REACH * 8, 4 * GRID)


def y_spans():
    cols = columns()
    spans = []
    for start in range(0, COLS, TILE):
        ks = [k for _, k in cols[start : start + TILE]]
        spans.append((min(ks) - 1, max(ks)))
    return spans


def y_constant():
    cos, sin = tables()
    out = np.zeros((2, GRID, 2, TILE), np.float64)
    for q in range(-REACH, REACH + 1):
        out[0, :, 0, q + REACH] = cos[:, q % GRID]
        out[0, :, 1, q + REACH] = sin[:, q % GRID]
        out[1, :, 0, q + REACH] = -sin[:, q % GRID]
        out[1, :, 1, q + REACH] = cos[:, q % GRID]
    return out.reshape(2, 2 * GRID, TILE)


def y_runs():
    cols = columns()
    runs = []
    for tile, (first, last) in enumerate(y_spans()):
        own = cols[tile * TILE : (tile + 1) * TILE]
        for k in range(first + 1, last + 1):
            lanes = [lane for lane, col in enumerate(own) if col[1] == k]
            q = own[lanes[0]][0]
            runs.append((lanes[0], lanes[-1] + 1, (q + REACH) % GRID))
    return runs


def x_constant():
    cos, sin = tables()
    out = np.zeros((2, PAIR_ROWS, GRID // 2, 2, 2, 2), np.float64)
    for pair in range(2):
        for a in range(-REACH, REACH + 1):
            c = cos[:, a % GRID].reshape(-1, 2)
            s = sin[:, a % GRID].reshape(-1, 2)
            out[pair, a + REACH, :, 0, pair] = c
            out[pair, a + REACH, :, 1, pair] = s
            out[pair, SIDE + a + REACH, :, 0, pair] = -s
            out[pair, SIDE + a + REACH, :, 1, pair] = c
    return out.reshape(2 * PAIR_ROWS, 4 * GRID)


def column_keys():
    keys = np.full((COLS, 1), -1, np.int32)
    for lane, (q, k) in enumerate(columns()):
        keys[lane, 0] = q * GRID + k
    return keys


def transform_kernel(
    val_hbm, cond_hbm, vi_hbm, ci_hbm, yq_hbm, zt_hbm, out_ref,
    val_ref, cond_ref, vi_ref, ci_ref, yq_ref, zt_ref, yt_ref, dens_ref, part_ref, sems,
):
    pairs = dens_ref.shape[0] // 2
    moves = [
        pltpu.make_async_copy(src, dst, sems.at[i])
        for i, (src, dst) in enumerate(
            (
                (yq_hbm, yq_ref),
                (val_hbm, val_ref),
                (cond_hbm, cond_ref),
                (vi_hbm, vi_ref),
                (ci_hbm, ci_ref),
                (zt_hbm, zt_ref),
            )
        )
    ]
    for move in moves:
        move.start()
    moves[0].wait()
    lane = lax.broadcasted_iota(jnp.int32, (2 * GRID, TILE), 1)
    for i, (first, last, place) in enumerate(y_runs()):
        inside = (lane >= first) & (lane < last)
        for out in range(2):
            moved = pltpu.roll(yq_ref[out], (first - place) % TILE, 1)
            yt_ref[2 * GRID * i : 2 * GRID * (i + 1), out * TILE : (out + 1) * TILE] = jnp.where(
                inside, moved, 0.0
            ).astype(BF16)
    first_pair = (
        (lax.axis_index("x") * 2 + lax.axis_index("z_lo")) * 2 + lax.axis_index("core")
    ) * pairs
    for move in moves[1:]:
        move.wait()
    for p in range(pairs):
        val = val_ref[vi_ref[first_pair + p]]
        cond = cond_ref[ci_ref[first_pair + p]]
        dens_ref[2 * p : 2 * p + 2, :] = val * cond
    for j in range(GRID // 4):
        zt = lax.dot_general(
            zt_ref[...],
            dens_ref[:, j * 256 : (j + 1) * 256],
            (((1,), (1,)), ((), ())),
            preferred_element_type=F32,
        )
        part_ref[:, j * 8 : (j + 1) * 8, :] = zt.reshape(REACH, 8, 2 * pairs)
    low = lax.broadcasted_iota(jnp.int32, (2 * pairs, TILE), 0) % 8 < 4
    row = 0
    for tile, (first, last) in enumerate(y_spans()):
        depth = (last - first) * 2 * GRID
        left = part_ref[first:last].astype(BF16).reshape(depth, 2 * pairs)
        both = lax.dot_general(
            left, yt_ref[row : row + depth, :], (((0,), (0,)), ((), ())), preferred_element_type=F32
        )
        row += depth
        real, imag = both[:, :TILE], both[:, TILE:]
        even = jnp.where(low, real, pltpu.roll(imag, 4, 0))
        odd = jnp.where(low, pltpu.roll(real, 2 * pairs - 4, 0), imag)
        for m in range(2 * pairs // 8):
            out_ref[16 * m : 16 * m + 16, tile * TILE : (tile + 1) * TILE] = jnp.concatenate(
                [even[8 * m : 8 * m + 8], odd[8 * m : 8 * m + 8]], 0
            ).astype(BF16)


def transform(pairs, val_index, cond_index, val_orbitals, cond_orbitals):
    hbm = pl.BlockSpec(memory_space=pltpu.HBM)
    y_table = jnp.asarray(jnp.asarray(y_constant(), BF16), F32)
    z_table = jnp.asarray(z_constant(), BF16)
    return pl.pallas_call(
        transform_kernel,
        out_shape=jax.ShapeDtypeStruct((4 * pairs, COLS), BF16),
        in_specs=[hbm] * 6,
        out_specs=pl.BlockSpec(memory_space=pltpu.VMEM),
        scratch_shapes=[
            pltpu.VMEM(val_orbitals.shape, BF16),
            pltpu.VMEM(cond_orbitals.shape, BF16),
            pltpu.SMEM(val_index.shape, jnp.int32),
            pltpu.SMEM(cond_index.shape, jnp.int32),
            pltpu.VMEM(y_table.shape, F32),
            pltpu.VMEM(z_table.shape, BF16),
            pltpu.VMEM((len(y_runs()) * 2 * GRID, 2 * TILE), BF16),
            pltpu.VMEM((2 * pairs, GRID * GRID), BF16),
            pltpu.VMEM((REACH, 2 * GRID, 2 * pairs), F32),
            pltpu.SemaphoreType.DMA((6,)),
        ],
        compiler_params=pltpu.CompilerParams(vmem_limit_bytes=VMEM_LIMIT),
        name="transform",
    )(val_orbitals, cond_orbitals, val_index, cond_index, y_table, z_table)


def select_kernel(y_ref, xt_ref, key_ref, gmap_ref, out_ref):
    spec = jnp.dot(xt_ref[...], y_ref[...], preferred_element_type=F32)
    spec = (spec * float(GRID) ** (-1.5)).astype(BF16)
    rows, _, width = gmap_ref.shape
    half = width // 2
    side = lax.broadcasted_iota(jnp.int32, (PAIR_ROWS, width), 0)
    for r in range(rows):
        entry = gmap_ref[r]
        key = entry & (GRID * GRID - 1)
        wave_a = (entry >> 12) & (GRID - 1)
        row = (entry >> 18) * SIDE + ((wave_a + REACH) & (GRID - 1))
        same = key_ref[...].astype(jnp.int16) == key.astype(jnp.int16)
        hit = jnp.where(same, jnp.asarray(1, BF16), jnp.asarray(0, BF16))
        found = jnp.dot(spec, hit, preferred_element_type=F32)
        here = side == row
        picked = [
            jnp.sum(jnp.where(here, found[i * PAIR_ROWS : (i + 1) * PAIR_ROWS], 0.0), 0, keepdims=True)
            for i in range(2)
        ]
        both = jnp.concatenate(picked, 0).astype(BF16)
        halves = both[:, :half], both[:, half:]
        for col in range(2 * rows):
            out_ref[r * 2 * rows + col, :, :half] = halves[col % 2]
        for which in range(2):
            col = 2 * r + which
            for other in range(rows):
                start = other % 2 * TILE
                out_ref[other * 2 * rows + col, :, half:] = halves[which][:, start : start + 2 * TILE]


def select(block, gmap, rows):
    width = NG // rows
    vmem = pl.BlockSpec(memory_space=pltpu.VMEM)
    return pl.pallas_call(
        select_kernel,
        out_shape=jax.ShapeDtypeStruct((2 * rows * rows, 2, width // 2 + 2 * TILE), BF16),
        in_specs=[vmem] * 4,
        out_specs=vmem,
        compiler_params=pltpu.CompilerParams(vmem_limit_bytes=32 * 2**20),
        name="select",
    )(block, jnp.asarray(x_constant(), BF16), jnp.asarray(column_keys()), gmap.reshape(rows, 1, width))


def half_product(left, right, weight_ref, out_ref, res_ref, sems, half):
    pairs, rows = left.shape
    turned = left.T.astype(F32)
    place = pl.ds(pl.multiple_of(half * rows, rows), rows)
    moves = []
    for f in range(weight_ref.shape[0]):
        weighted = (turned * weight_ref[f : f + 1, :]).astype(BF16)
        total = jnp.dot(weighted, right, preferred_element_type=F32)
        res_ref[f] = total * (1.0 / math.sqrt(pairs))
        moves.append(pltpu.make_async_copy(res_ref.at[f], out_ref.at[f, place], sems.at[f]))
        moves[-1].start()
    for move in moves:
        move.wait()


def own_kernel(mine_ref, thirds_ref, weight_ref, out_ref, right_ref, res_ref, sems):
    pairs = right_ref.shape[0]
    half = mine_ref.shape[2] - 2 * TILE
    core = lax.axis_index("core")
    here = pl.ds(pl.multiple_of(core * TILE, TILE), 2 * TILE)
    there = pl.ds(pl.multiple_of((1 - core) * 2 * TILE, TILE), TILE)
    right_ref[:, here] = mine_ref[:, :, half:].reshape(pairs, 2 * TILE)
    right_ref[:, there] = thirds_ref[1 - core].reshape(pairs, TILE)
    left = mine_ref[:, :, :half].reshape(pairs, half)
    half_product(left, right_ref[...], weight_ref, out_ref, res_ref, sems, lax.axis_index("y") % 2)


def rest_kernel(low_ref, high_ref, right_ref, weight_ref, begun_ref, out_ref, res_ref, sems):
    part, _, half = low_ref.shape
    left = jnp.concatenate(
        [low_ref[...].reshape(2 * part, half), high_ref[...].reshape(2 * part, half)], 0
    )
    half_product(left, right_ref[...], weight_ref, out_ref, res_ref, sems, 1 - lax.axis_index("y") % 2)


def half_call(kernel, name, in_specs, out_shape, out_specs, half, width, aliases):
    work = 2 * 2 * PAIRS * half * width
    return pl.pallas_call(
        kernel,
        out_shape=out_shape,
        in_specs=in_specs,
        out_specs=out_specs,
        scratch_shapes=[pltpu.VMEM((2, half, width), F32), pltpu.SemaphoreType.DMA((2,))],
        input_output_aliases=aliases,
        cost_estimate=pl.CostEstimate(flops=work, bytes_accessed=5 * 2**20, transcendentals=0),
        compiler_params=pltpu.CompilerParams(vmem_limit_bytes=32 * 2**20),
        name=name,
    )


def own_product(mine, thirds, weights, rows, width):
    vmem = pl.BlockSpec(memory_space=pltpu.VMEM)
    hbm = pl.BlockSpec(memory_space=pltpu.HBM)
    shapes = (
        jax.ShapeDtypeStruct((weights.shape[0], rows, width), F32),
        jax.ShapeDtypeStruct((PAIRS, width), BF16),
    )
    call = half_call(own_kernel, "own_half", [vmem] * 3, shapes, (hbm, vmem), rows // 2, width, {})
    return call(mine, thirds, weights)


def rest_product(low, high, right, weights, begun):
    vmem = pl.BlockSpec(memory_space=pltpu.VMEM)
    hbm = pl.BlockSpec(memory_space=pltpu.HBM)
    _, rows, width = begun.shape
    shape = jax.ShapeDtypeStruct(begun.shape, F32)
    specs = [vmem] * 4 + [hbm]
    call = half_call(rest_kernel, "other_half", specs, shape, hbm, rows // 2, width, {4: 0})
    return call(low, high, right, weights, begun)


def pair_weights(val_index, cond_index, val_energy, cond_energy, freqs):
    val_hit = val_index[:, None] == jnp.arange(val_energy.shape[0], dtype=jnp.int32)[None, :]
    cond_hit = cond_index[:, None] == jnp.arange(cond_energy.shape[0], dtype=jnp.int32)[None, :]
    gap = jnp.sum(jnp.where(cond_hit, cond_energy[None, :], 0.0), 1) - jnp.sum(
        jnp.where(val_hit, val_energy[None, :], 0.0), 1
    )
    return -4.0 * gap[None, :] / (gap[None, :] ** 2 + freqs[:, None] ** 2)


ROW = ("x", "z_lo", "core")
COL = ("z_hi", "y")


def shards(
    val_orbitals, cond_orbitals, val_index, cond_index, val_energy, cond_energy, freqs, gmap
):
    row_count = lax.axis_size(ROW)
    col_count = lax.axis_size(COL)
    pair_dev = val_index.shape[0] // row_count
    partial = transform(pair_dev, val_index, cond_index, val_orbitals, cond_orbitals)
    block = lax.all_to_all(
        partial.reshape(col_count, 8, COLS), COL, split_axis=0, concat_axis=0, tiled=True
    ).reshape(4 * GRID, COLS)
    mine = lax.all_to_all(
        select(block, gmap, row_count), ROW + COL, split_axis=0, concat_axis=0, tiled=True
    )
    sources = mine.shape[0] // 2
    rows, width = NG // row_count, NG // col_count
    half = rows // 2
    count = lax.axis_size("y")
    low = lax.ppermute(mine[:sources, :, :half], "y", [((i + 1) % count, i) for i in range(count)])
    high = lax.ppermute(mine[sources:, :, :half], "y", [(i, (i + 1) % count) for i in range(count)])
    third = lax.dynamic_slice(
        mine, (0, 0, half + lax.axis_index("core") * TILE), (2 * sources, 2, TILE)
    )
    thirds = lax.all_gather(third, "core")
    weights = pair_weights(val_index, cond_index, val_energy, cond_energy, freqs)
    begun, right = own_product(mine, thirds, weights, rows, width)
    return rest_product(low, high, right, weights, begun)


def solution(mesh):
    fine = Mesh(mesh.devices.reshape(4, 2, 2, 4, 8), ROW + COL)
    orbitals = P(None, COL, None)
    placed = (orbitals, orbitals, P(), P(), P(), P(), P(), P())
    return jax.shard_map(
        shards, mesh=fine, in_specs=placed, out_specs=P(None, ROW, COL), check_vma=False
    )
```

```python
import functools
import math

import jax
import jax.numpy as jnp
import numpy as np
from jax import lax
from jax.experimental import pallas as pl
from jax.experimental.pallas import tpu as pltpu
from jax.sharding import Mesh, PartitionSpec as P

GRID = 64
NG = 12288
PAIRS = 1024
REACH = 18
SIDE = 2 * REACH + 1
RADIUS2 = 334
COLS = 512
PAIR_ROWS = 80
TILE = 128
BF16 = jnp.bfloat16
F32 = jnp.float32
VMEM_LIMIT = 60 * 2**20


def tables():
    idx = np.arange(GRID)
    phase = (idx[:, None] * idx[None, :] % GRID).astype(np.float32) * np.float32(2.0 * math.pi / GRID)
    phase = phase.astype(np.float64)
    return np.cos(phase), np.sin(phase)


def columns():
    found = []
    for k in range(1, REACH + 1):
        for q in range(-REACH, REACH + 1):
            if q * q + k * k <= RADIUS2:
                found.append((q % GRID, k))
    return found


def z_constant():
    cos, sin = tables()
    out = np.zeros((REACH, 4, 2, 4, GRID), np.float64)
    for k in range(1, REACH + 1):
        for y in range(4):
            out[k - 1, y, 0, y] = cos[:, k]
            out[k - 1, y, 1, y] = -sin[:, k]
    return out.reshape(REACH * 8, 4 * GRID)


def y_spans():
    cols = columns()
    spans = []
    for start in range(0, COLS, TILE):
        ks = [k for _, k in cols[start : start + TILE]]
        spans.append((min(ks) - 1, max(ks)))
    return spans


def y_constant():
    cos, sin = tables()
    out = np.zeros((2, GRID, 2, TILE), np.float64)
    for q in range(-REACH, REACH + 1):
        out[0, :, 0, q + REACH] = cos[:, q % GRID]
        out[0, :, 1, q + REACH] = sin[:, q % GRID]
        out[1, :, 0, q + REACH] = -sin[:, q % GRID]
        out[1, :, 1, q + REACH] = cos[:, q % GRID]
    return out.reshape(2, 2 * GRID, TILE)


def y_runs():
    cols = columns()
    runs = []
    for tile, (first, last) in enumerate(y_spans()):
        own = cols[tile * TILE : (tile + 1) * TILE]
        for k in range(first + 1, last + 1):
            lanes = [lane for lane, col in enumerate(own) if col[1] == k]
            q = own[lanes[0]][0]
            runs.append((lanes[0], lanes[-1] + 1, (q + REACH) % GRID))
    return runs


def x_constant():
    cos, sin = tables()
    out = np.zeros((2, PAIR_ROWS, GRID // 2, 2, 2, 2), np.float64)
    for pair in range(2):
        for a in range(-REACH, REACH + 1):
            c = cos[:, a % GRID].reshape(-1, 2)
            s = sin[:, a % GRID].reshape(-1, 2)
            out[pair, a + REACH, :, 0, pair] = c
            out[pair, a + REACH, :, 1, pair] = s
            out[pair, SIDE + a + REACH, :, 0, pair] = -s
            out[pair, SIDE + a + REACH, :, 1, pair] = c
    return out.reshape(2 * PAIR_ROWS, 4 * GRID)


def column_keys():
    keys = np.full((COLS, 1), -1, np.int32)
    for lane, (q, k) in enumerate(columns()):
        keys[lane, 0] = q * GRID + k
    return keys


def transform_kernel(
    val_hbm, cond_hbm, vi_hbm, ci_hbm, yq_hbm, zt_hbm, out_ref,
    val_ref, cond_ref, vi_ref, ci_ref, yq_ref, zt_ref, yt_ref, dens_ref, part_ref, sems,
):
    pairs = dens_ref.shape[0] // 2
    moves = [
        pltpu.make_async_copy(src, dst, sems.at[i])
        for i, (src, dst) in enumerate(
            (
                (yq_hbm, yq_ref),
                (val_hbm, val_ref),
                (cond_hbm, cond_ref),
                (vi_hbm, vi_ref),
                (ci_hbm, ci_ref),
                (zt_hbm, zt_ref),
            )
        )
    ]
    for move in moves:
        move.start()
    moves[0].wait()
    lane = lax.broadcasted_iota(jnp.int32, (2 * GRID, TILE), 1)
    for i, (first, last, place) in enumerate(y_runs()):
        inside = (lane >= first) & (lane < last)
        for out in range(2):
            moved = pltpu.roll(yq_ref[out], (first - place) % TILE, 1)
            yt_ref[2 * GRID * i : 2 * GRID * (i + 1), out * TILE : (out + 1) * TILE] = jnp.where(
                inside, moved, 0.0
            ).astype(BF16)
    first_pair = (
        (lax.axis_index("x") * 2 + lax.axis_index("z_lo")) * 2 + lax.axis_index("core")
    ) * pairs
    for move in moves[1:]:
        move.wait()
    for p in range(pairs):
        val = val_ref[vi_ref[first_pair + p]]
        cond = cond_ref[ci_ref[first_pair + p]]
        dens_ref[2 * p : 2 * p + 2, :] = val * cond
    for j in range(GRID // 4):
        zt = lax.dot_general(
            zt_ref[...],
            dens_ref[:, j * 256 : (j + 1) * 256],
            (((1,), (1,)), ((), ())),
            preferred_element_type=F32,
        )
        part_ref[:, j * 8 : (j + 1) * 8, :] = zt.reshape(REACH, 8, 2 * pairs)
    low = lax.broadcasted_iota(jnp.int32, (2 * pairs, TILE), 0) % 8 < 4
    row = 0
    for tile, (first, last) in enumerate(y_spans()):
        depth = (last - first) * 2 * GRID
        left = part_ref[first:last].astype(BF16).reshape(depth, 2 * pairs)
        both = lax.dot_general(
            left, yt_ref[row : row + depth, :], (((0,), (0,)), ((), ())), preferred_element_type=F32
        )
        row += depth
        real, imag = both[:, :TILE], both[:, TILE:]
        even = jnp.where(low, real, pltpu.roll(imag, 4, 0))
        odd = jnp.where(low, pltpu.roll(real, 2 * pairs - 4, 0), imag)
        for m in range(2 * pairs // 8):
            out_ref[16 * m : 16 * m + 16, tile * TILE : (tile + 1) * TILE] = jnp.concatenate(
                [even[8 * m : 8 * m + 8], odd[8 * m : 8 * m + 8]], 0
            ).astype(BF16)


def transform(pairs, val_index, cond_index, val_orbitals, cond_orbitals):
    hbm = pl.BlockSpec(memory_space=pltpu.HBM)
    y_table = jnp.asarray(jnp.asarray(y_constant(), BF16), F32)
    z_table = jnp.asarray(z_constant(), BF16)
    return pl.pallas_call(
        transform_kernel,
        out_shape=jax.ShapeDtypeStruct((4 * pairs, COLS), BF16),
        in_specs=[hbm] * 6,
        out_specs=pl.BlockSpec(memory_space=pltpu.VMEM),
        scratch_shapes=[
            pltpu.VMEM(val_orbitals.shape, BF16),
            pltpu.VMEM(cond_orbitals.shape, BF16),
            pltpu.SMEM(val_index.shape, jnp.int32),
            pltpu.SMEM(cond_index.shape, jnp.int32),
            pltpu.VMEM(y_table.shape, F32),
            pltpu.VMEM(z_table.shape, BF16),
            pltpu.VMEM((len(y_runs()) * 2 * GRID, 2 * TILE), BF16),
            pltpu.VMEM((2 * pairs, GRID * GRID), BF16),
            pltpu.VMEM((REACH, 2 * GRID, 2 * pairs), F32),
            pltpu.SemaphoreType.DMA((6,)),
        ],
        compiler_params=pltpu.CompilerParams(vmem_limit_bytes=VMEM_LIMIT),
        name="transform",
    )(val_orbitals, cond_orbitals, val_index, cond_index, y_table, z_table)


def select_kernel(y_ref, xt_ref, key_ref, gmap_ref, out_ref):
    spec = jnp.dot(xt_ref[...], y_ref[...], preferred_element_type=F32)
    spec = (spec * float(GRID) ** (-1.5)).astype(BF16)
    rows, _, width = gmap_ref.shape
    half = width // 2
    side = lax.broadcasted_iota(jnp.int32, (PAIR_ROWS, width), 0)
    for r in range(rows):
        entry = gmap_ref[r]
        key = entry & (GRID * GRID - 1)
        wave_a = (entry >> 12) & (GRID - 1)
        row = (entry >> 18) * SIDE + ((wave_a + REACH) & (GRID - 1))
        same = key_ref[...].astype(jnp.int16) == key.astype(jnp.int16)
        hit = jnp.where(same, jnp.asarray(1, BF16), jnp.asarray(0, BF16))
        found = jnp.dot(spec, hit, preferred_element_type=F32)
        here = side == row
        picked = [
            jnp.sum(jnp.where(here, found[i * PAIR_ROWS : (i + 1) * PAIR_ROWS], 0.0), 0, keepdims=True)
            for i in range(2)
        ]
        both = jnp.concatenate(picked, 0).astype(BF16)
        halves = both[:, :half], both[:, half:]
        for col in range(2 * rows):
            out_ref[r * 2 * rows + col, :, :half] = halves[col % 2]
        for which in range(2):
            col = 2 * r + which
            for other in range(rows):
                third = other % 2 if other // 2 % 2 == 0 else 2
                out_ref[other * 2 * rows + col, :, half:] = halves[which][
                    :, third * TILE : (third + 1) * TILE
                ]


def select(block, gmap, rows):
    width = NG // rows
    vmem = pl.BlockSpec(memory_space=pltpu.VMEM)
    return pl.pallas_call(
        select_kernel,
        out_shape=jax.ShapeDtypeStruct((2 * rows * rows, 2, width // 2 + TILE), BF16),
        in_specs=[vmem] * 4,
        out_specs=vmem,
        compiler_params=pltpu.CompilerParams(vmem_limit_bytes=32 * 2**20),
        name="select",
    )(block, jnp.asarray(x_constant(), BF16), jnp.asarray(column_keys()), gmap.reshape(rows, 1, width))


def half_product(left, right, weight_ref, out_ref, res_ref, sems, half):
    pairs, rows = left.shape
    turned = left.T.astype(F32)
    place = pl.ds(pl.multiple_of(half * rows, rows), rows)
    moves = []
    for f in range(weight_ref.shape[0]):
        weighted = (turned * weight_ref[f : f + 1, :]).astype(BF16)
        total = jnp.dot(weighted, right, preferred_element_type=F32)
        res_ref[f] = total * (1.0 / math.sqrt(pairs))
        moves.append(pltpu.make_async_copy(res_ref.at[f], out_ref.at[f, place], sems.at[f]))
        moves[-1].start()
    for move in moves:
        move.wait()


def own_kernel(mine_ref, zs_ref, cores_ref, weight_ref, out_ref, right_ref, res_ref, sems):
    pairs = right_ref.shape[0]
    half = mine_ref.shape[2] - TILE
    for third, value in enumerate((cores_ref[0], cores_ref[1], zs_ref[1])):
        right_ref[:, third * TILE : (third + 1) * TILE] = value.reshape(pairs, TILE)
    left = mine_ref[:, :, :half].reshape(pairs, half)
    half_product(left, right_ref[...], weight_ref, out_ref, res_ref, sems, lax.axis_index("y") % 2)


def rest_kernel(low_ref, high_ref, right_ref, weight_ref, begun_ref, out_ref, res_ref, sems):
    part, _, half = low_ref.shape
    left = jnp.concatenate(
        [low_ref[...].reshape(2 * part, half), high_ref[...].reshape(2 * part, half)], 0
    )
    half_product(left, right_ref[...], weight_ref, out_ref, res_ref, sems, 1 - lax.axis_index("y") % 2)


def half_call(kernel, name, in_specs, out_shape, out_specs, half, width, aliases):
    work = 2 * 2 * PAIRS * half * width
    return pl.pallas_call(
        kernel,
        out_shape=out_shape,
        in_specs=in_specs,
        out_specs=out_specs,
        scratch_shapes=[pltpu.VMEM((2, half, width), F32), pltpu.SemaphoreType.DMA((2,))],
        input_output_aliases=aliases,
        cost_estimate=pl.CostEstimate(flops=work, bytes_accessed=5 * 2**20, transcendentals=0),
        compiler_params=pltpu.CompilerParams(vmem_limit_bytes=32 * 2**20),
        name=name,
    )


def own_product(mine, by_z, by_core, weights, rows, width):
    vmem = pl.BlockSpec(memory_space=pltpu.VMEM)
    hbm = pl.BlockSpec(memory_space=pltpu.HBM)
    shapes = (
        jax.ShapeDtypeStruct((weights.shape[0], rows, width), F32),
        jax.ShapeDtypeStruct((PAIRS, width), BF16),
    )
    call = half_call(own_kernel, "own_half", [vmem] * 4, shapes, (hbm, vmem), rows // 2, width, {})
    return call(mine, by_z, by_core, weights)


def rest_product(low, high, right, weights, begun):
    vmem = pl.BlockSpec(memory_space=pltpu.VMEM)
    hbm = pl.BlockSpec(memory_space=pltpu.HBM)
    _, rows, width = begun.shape
    shape = jax.ShapeDtypeStruct(begun.shape, F32)
    specs = [vmem] * 4 + [hbm]
    call = half_call(rest_kernel, "other_half", specs, shape, hbm, rows // 2, width, {4: 0})
    return call(low, high, right, weights, begun)


def pair_weights(val_index, cond_index, val_energy, cond_energy, freqs):
    val_hit = val_index[:, None] == jnp.arange(val_energy.shape[0], dtype=jnp.int32)[None, :]
    cond_hit = cond_index[:, None] == jnp.arange(cond_energy.shape[0], dtype=jnp.int32)[None, :]
    gap = jnp.sum(jnp.where(cond_hit, cond_energy[None, :], 0.0), 1) - jnp.sum(
        jnp.where(val_hit, val_energy[None, :], 0.0), 1
    )
    return -4.0 * gap[None, :] / (gap[None, :] ** 2 + freqs[:, None] ** 2)


ROW = ("x", "z_lo", "core")
COL = ("z_hi", "y")


def shards(
    val_orbitals, cond_orbitals, val_index, cond_index, val_energy, cond_energy, freqs, gmap
):
    row_count = lax.axis_size(ROW)
    col_count = lax.axis_size(COL)
    pair_dev = val_index.shape[0] // row_count
    partial = transform(pair_dev, val_index, cond_index, val_orbitals, cond_orbitals)
    block = lax.all_to_all(
        partial.reshape(col_count, 8, COLS), COL, split_axis=0, concat_axis=0, tiled=True
    ).reshape(4 * GRID, COLS)
    mine = lax.all_to_all(
        select(block, gmap, row_count), ROW + COL, split_axis=0, concat_axis=0, tiled=True
    )
    sources = mine.shape[0] // 2
    rows, width = NG // row_count, NG // col_count
    half = rows // 2
    count = lax.axis_size("y")
    low = lax.ppermute(mine[:sources, :, :half], "y", [((i + 1) % count, i) for i in range(count)])
    high = lax.ppermute(mine[sources:, :, :half], "y", [(i, (i + 1) % count) for i in range(count)])
    by_z = lax.all_gather(mine[:, :, half:], "z_lo")
    by_core = lax.all_gather(by_z[0], "core")
    weights = pair_weights(val_index, cond_index, val_energy, cond_energy, freqs)
    begun, right = own_product(mine, by_z, by_core, weights, rows, width)
    return rest_product(low, high, right, weights, begun)


def solution(mesh):
    fine = Mesh(mesh.devices.reshape(4, 2, 2, 4, 8), ROW + COL)
    orbitals = P(None, COL, None)
    placed = (orbitals, orbitals, P(), P(), P(), P(), P(), P())
    return jax.shard_map(
        shards, mesh=fine, in_specs=placed, out_specs=P(None, ROW, COL), check_vma=False
    )
```

```python
import functools
import math

import jax
import jax.numpy as jnp
import numpy as np
from jax import lax
from jax.experimental import pallas as pl
from jax.experimental.pallas import tpu as pltpu
from jax.sharding import Mesh, PartitionSpec as P

GRID = 64
NG = 12288
PAIRS = 1024
REACH = 18
SIDE = 2 * REACH + 1
RADIUS2 = 334
COLS = 512
PAIR_ROWS = 80
TILE = 128
BF16 = jnp.bfloat16
F32 = jnp.float32
VMEM_LIMIT = 60 * 2**20


def tables():
    idx = np.arange(GRID)
    phase = (idx[:, None] * idx[None, :] % GRID).astype(np.float32) * np.float32(2.0 * math.pi / GRID)
    phase = phase.astype(np.float64)
    return np.cos(phase), np.sin(phase)


def columns():
    found = []
    for k in range(1, REACH + 1):
        for q in range(-REACH, REACH + 1):
            if q * q + k * k <= RADIUS2:
                found.append((q % GRID, k))
    return found


def z_constant():
    cos, sin = tables()
    out = np.zeros((REACH, 4, 2, 4, GRID), np.float64)
    for k in range(1, REACH + 1):
        for y in range(4):
            out[k - 1, y, 0, y] = cos[:, k]
            out[k - 1, y, 1, y] = -sin[:, k]
    return out.reshape(REACH * 8, 4 * GRID)


def y_spans():
    cols = columns()
    spans = []
    for start in range(0, COLS, TILE):
        ks = [k for _, k in cols[start : start + TILE]]
        spans.append((min(ks) - 1, max(ks)))
    return spans


def y_constant():
    cos, sin = tables()
    out = np.zeros((2, GRID, 2, TILE), np.float64)
    for q in range(-REACH, REACH + 1):
        out[0, :, 0, q + REACH] = cos[:, q % GRID]
        out[0, :, 1, q + REACH] = sin[:, q % GRID]
        out[1, :, 0, q + REACH] = -sin[:, q % GRID]
        out[1, :, 1, q + REACH] = cos[:, q % GRID]
    return out.reshape(2, 2 * GRID, TILE)


def y_runs():
    cols = columns()
    runs = []
    for tile, (first, last) in enumerate(y_spans()):
        own = cols[tile * TILE : (tile + 1) * TILE]
        for k in range(first + 1, last + 1):
            lanes = [lane for lane, col in enumerate(own) if col[1] == k]
            q = own[lanes[0]][0]
            runs.append((lanes[0], lanes[-1] + 1, (q + REACH) % GRID))
    return runs


def x_constant():
    cos, sin = tables()
    out = np.zeros((2, PAIR_ROWS, GRID // 2, 2, 2, 2), np.float64)
    for pair in range(2):
        for a in range(-REACH, REACH + 1):
            c = cos[:, a % GRID].reshape(-1, 2)
            s = sin[:, a % GRID].reshape(-1, 2)
            out[pair, a + REACH, :, 0, pair] = c
            out[pair, a + REACH, :, 1, pair] = s
            out[pair, SIDE + a + REACH, :, 0, pair] = -s
            out[pair, SIDE + a + REACH, :, 1, pair] = c
    return out.reshape(2 * PAIR_ROWS, 4 * GRID)


def column_keys():
    keys = np.full((COLS, 1), -1, np.int32)
    for lane, (q, k) in enumerate(columns()):
        keys[lane, 0] = q * GRID + k
    return keys


def transform_kernel(
    val_hbm, cond_hbm, vi_hbm, ci_hbm, yq_hbm, zt_hbm, out_ref,
    val_ref, cond_ref, vi_ref, ci_ref, yq_ref, zt_ref, yt_ref, dens_ref, part_ref, sems,
):
    pairs = dens_ref.shape[0] // 2
    moves = [
        pltpu.make_async_copy(src, dst, sems.at[i])
        for i, (src, dst) in enumerate(
            (
                (yq_hbm, yq_ref),
                (val_hbm, val_ref),
                (cond_hbm, cond_ref),
                (vi_hbm, vi_ref),
                (ci_hbm, ci_ref),
                (zt_hbm, zt_ref),
            )
        )
    ]
    for move in moves:
        move.start()
    moves[0].wait()
    lane = lax.broadcasted_iota(jnp.int32, (2 * GRID, TILE), 1)
    for i, (first, last, place) in enumerate(y_runs()):
        inside = (lane >= first) & (lane < last)
        for out in range(2):
            moved = pltpu.roll(yq_ref[out], (first - place) % TILE, 1)
            yt_ref[2 * GRID * i : 2 * GRID * (i + 1), out * TILE : (out + 1) * TILE] = jnp.where(
                inside, moved, 0.0
            ).astype(BF16)
    first_pair = (
        (lax.axis_index("x") * 2 + lax.axis_index("z_lo")) * 2 + lax.axis_index("core")
    ) * pairs
    for move in moves[1:]:
        move.wait()
    for p in range(pairs):
        val = val_ref[vi_ref[first_pair + p]]
        cond = cond_ref[ci_ref[first_pair + p]]
        dens_ref[2 * p : 2 * p + 2, :] = val * cond
    for j in range(GRID // 4):
        zt = lax.dot_general(
            zt_ref[...],
            dens_ref[:, j * 256 : (j + 1) * 256],
            (((1,), (1,)), ((), ())),
            preferred_element_type=F32,
        )
        part_ref[:, j * 8 : (j + 1) * 8, :] = zt.reshape(REACH, 8, 2 * pairs)
    low = lax.broadcasted_iota(jnp.int32, (2 * pairs, TILE), 0) % 8 < 4
    row = 0
    for tile, (first, last) in enumerate(y_spans()):
        depth = (last - first) * 2 * GRID
        left = part_ref[first:last].astype(BF16).reshape(depth, 2 * pairs)
        both = lax.dot_general(
            left, yt_ref[row : row + depth, :], (((0,), (0,)), ((), ())), preferred_element_type=F32
        )
        row += depth
        real, imag = both[:, :TILE], both[:, TILE:]
        even = jnp.where(low, real, pltpu.roll(imag, 4, 0))
        odd = jnp.where(low, pltpu.roll(real, 2 * pairs - 4, 0), imag)
        for m in range(2 * pairs // 8):
            out_ref[16 * m : 16 * m + 16, tile * TILE : (tile + 1) * TILE] = jnp.concatenate(
                [even[8 * m : 8 * m + 8], odd[8 * m : 8 * m + 8]], 0
            ).astype(BF16)


def transform(pairs, val_index, cond_index, val_orbitals, cond_orbitals):
    hbm = pl.BlockSpec(memory_space=pltpu.HBM)
    y_table = jnp.asarray(jnp.asarray(y_constant(), BF16), F32)
    z_table = jnp.asarray(z_constant(), BF16)
    return pl.pallas_call(
        transform_kernel,
        out_shape=jax.ShapeDtypeStruct((4 * pairs, COLS), BF16),
        in_specs=[hbm] * 6,
        out_specs=pl.BlockSpec(memory_space=pltpu.VMEM),
        scratch_shapes=[
            pltpu.VMEM(val_orbitals.shape, BF16),
            pltpu.VMEM(cond_orbitals.shape, BF16),
            pltpu.SMEM(val_index.shape, jnp.int32),
            pltpu.SMEM(cond_index.shape, jnp.int32),
            pltpu.VMEM(y_table.shape, F32),
            pltpu.VMEM(z_table.shape, BF16),
            pltpu.VMEM((len(y_runs()) * 2 * GRID, 2 * TILE), BF16),
            pltpu.VMEM((2 * pairs, GRID * GRID), BF16),
            pltpu.VMEM((REACH, 2 * GRID, 2 * pairs), F32),
            pltpu.SemaphoreType.DMA((6,)),
        ],
        compiler_params=pltpu.CompilerParams(vmem_limit_bytes=VMEM_LIMIT),
        name="transform",
    )(val_orbitals, cond_orbitals, val_index, cond_index, y_table, z_table)


def select_kernel(y_ref, xt_ref, key_ref, gmap_ref, out_ref):
    spec = jnp.dot(xt_ref[...], y_ref[...], preferred_element_type=F32)
    spec = (spec * float(GRID) ** (-1.5)).astype(BF16)
    rows, _, width = gmap_ref.shape
    half = width // 2
    side = lax.broadcasted_iota(jnp.int32, (PAIR_ROWS, width), 0)
    for r in range(rows):
        entry = gmap_ref[r]
        key = entry & (GRID * GRID - 1)
        wave_a = (entry >> 12) & (GRID - 1)
        row = (entry >> 18) * SIDE + ((wave_a + REACH) & (GRID - 1))
        same = key_ref[...].astype(jnp.int16) == key.astype(jnp.int16)
        hit = jnp.where(same, jnp.asarray(1, BF16), jnp.asarray(0, BF16))
        found = jnp.dot(spec, hit, preferred_element_type=F32)
        here = side == row
        picked = [
            jnp.sum(jnp.where(here, found[i * PAIR_ROWS : (i + 1) * PAIR_ROWS], 0.0), 0, keepdims=True)
            for i in range(2)
        ]
        both = jnp.concatenate(picked, 0).astype(BF16)
        halves = both[:, :half], both[:, half:]
        for col in range(2 * rows):
            out_ref[r * 2 * rows + col, :, :half] = halves[col % 2]
        for which in range(2):
            col = 2 * r + which
            for other in range(rows):
                third = other % 2 if other // 2 % 2 == 0 else 2
                out_ref[other * 2 * rows + col, :, half:] = halves[which][
                    :, third * TILE : (third + 1) * TILE
                ]


def select(block, gmap, rows):
    width = NG // rows
    vmem = pl.BlockSpec(memory_space=pltpu.VMEM)
    return pl.pallas_call(
        select_kernel,
        out_shape=jax.ShapeDtypeStruct((2 * rows * rows, 2, width // 2 + TILE), BF16),
        in_specs=[vmem] * 4,
        out_specs=vmem,
        compiler_params=pltpu.CompilerParams(vmem_limit_bytes=32 * 2**20),
        name="select",
    )(block, jnp.asarray(x_constant(), BF16), jnp.asarray(column_keys()), gmap.reshape(rows, 1, width))


def product_kernel(
    mine_ref, low_ref, high_ref, zs_ref, cores_ref, weight_ref, out_ref, right_ref, res_ref, sems
):
    pairs = right_ref.shape[0]
    half = mine_ref.shape[2] - TILE
    freqs = weight_ref.shape[0]
    for third, value in enumerate((cores_ref[0], cores_ref[1], zs_ref[1])):
        right_ref[:, third * TILE : (third + 1) * TILE] = value.reshape(pairs, TILE)
    right = right_ref[...]
    own = lax.axis_index("y") % 2
    moves = []
    for step in range(2):
        if step == 0:
            left = mine_ref[:, :, :half].reshape(pairs, half)
        else:
            part = (pairs // 2, half)
            left = jnp.concatenate([low_ref[...].reshape(part), high_ref[...].reshape(part)], 0)
        place = own if step == 0 else 1 - own
        place = pl.ds(pl.multiple_of(place * half, half), half)
        turned = left.T.astype(F32)
        for f in range(freqs):
            weighted = (turned * weight_ref[f : f + 1, :]).astype(BF16)
            total = jnp.dot(weighted, right, preferred_element_type=F32)
            res_ref[step, f] = total * (1.0 / math.sqrt(pairs))
            moves.append(
                pltpu.make_async_copy(
                    res_ref.at[step, f], out_ref.at[f, place], sems.at[step * freqs + f]
                )
            )
            moves[-1].start()
    for move in moves:
        move.wait()


def product(mine, low, high, by_z, by_core, weights, rows, width):
    freqs = weights.shape[0]
    return pl.pallas_call(
        product_kernel,
        out_shape=jax.ShapeDtypeStruct((freqs, rows, width), F32),
        in_specs=[pl.BlockSpec(memory_space=pltpu.VMEM)] * 6,
        out_specs=pl.BlockSpec(memory_space=pltpu.HBM),
        scratch_shapes=[
            pltpu.VMEM((PAIRS, width), BF16),
            pltpu.VMEM((2, freqs, rows // 2, width), F32),
            pltpu.SemaphoreType.DMA((2 * freqs,)),
        ],
        compiler_params=pltpu.CompilerParams(vmem_limit_bytes=32 * 2**20),
        name="product",
    )(mine, low, high, by_z, by_core, weights)


def pair_weights(val_index, cond_index, val_energy, cond_energy, freqs):
    val_hit = val_index[:, None] == jnp.arange(val_energy.shape[0], dtype=jnp.int32)[None, :]
    cond_hit = cond_index[:, None] == jnp.arange(cond_energy.shape[0], dtype=jnp.int32)[None, :]
    gap = jnp.sum(jnp.where(cond_hit, cond_energy[None, :], 0.0), 1) - jnp.sum(
        jnp.where(val_hit, val_energy[None, :], 0.0), 1
    )
    return -4.0 * gap[None, :] / (gap[None, :] ** 2 + freqs[:, None] ** 2)


ROW = ("x", "z_lo", "core")
COL = ("z_hi", "y")


def shards(
    val_orbitals, cond_orbitals, val_index, cond_index, val_energy, cond_energy, freqs, gmap
):
    row_count = lax.axis_size(ROW)
    col_count = lax.axis_size(COL)
    pair_dev = val_index.shape[0] // row_count
    partial = transform(pair_dev, val_index, cond_index, val_orbitals, cond_orbitals)
    block = lax.all_to_all(
        partial.reshape(col_count, 8, COLS), COL, split_axis=0, concat_axis=0, tiled=True
    ).reshape(4 * GRID, COLS)
    mine = lax.all_to_all(
        select(block, gmap, row_count), ROW + COL, split_axis=0, concat_axis=0, tiled=True
    )
    weights = pair_weights(val_index, cond_index, val_energy, cond_energy, freqs)
    mine, weights = lax.optimization_barrier((mine, weights))
    sources = mine.shape[0] // 2
    rows, width = NG // row_count, NG // col_count
    half = rows // 2
    count = lax.axis_size("y")
    low = lax.ppermute(mine[:sources, :, :half], "y", [((i + 1) % count, i) for i in range(count)])
    high = lax.ppermute(mine[sources:, :, :half], "y", [(i, (i + 1) % count) for i in range(count)])
    by_z = lax.all_gather(mine[:, :, half:], "z_lo")
    by_core = lax.all_gather(by_z[0], "core")
    return product(mine, low, high, by_z, by_core, weights, rows, width)


def solution(mesh):
    fine = Mesh(mesh.devices.reshape(4, 2, 2, 4, 8), ROW + COL)
    orbitals = P(None, COL, None)
    placed = (orbitals, orbitals, P(), P(), P(), P(), P(), P())
    return jax.shard_map(
        shards, mesh=fine, in_specs=placed, out_specs=P(None, ROW, COL), check_vma=False
    )
```

```python
import functools
import math

import jax
import jax.numpy as jnp
import numpy as np
from jax import lax
from jax.experimental import pallas as pl
from jax.experimental.pallas import tpu as pltpu
from jax.sharding import Mesh, PartitionSpec as P

GRID = 64
NG = 12288
PAIRS = 1024
REACH = 18
SIDE = 2 * REACH + 1
RADIUS2 = 334
COLS = 512
PAIR_ROWS = 80
TILE = 128
BF16 = jnp.bfloat16
F32 = jnp.float32
VMEM_LIMIT = 60 * 2**20


def tables():
    idx = np.arange(GRID)
    phase = (idx[:, None] * idx[None, :] % GRID).astype(np.float32) * np.float32(2.0 * math.pi / GRID)
    phase = phase.astype(np.float64)
    return np.cos(phase), np.sin(phase)


def columns():
    found = []
    for k in range(1, REACH + 1):
        for q in range(-REACH, REACH + 1):
            if q * q + k * k <= RADIUS2:
                found.append((q % GRID, k))
    return found


def z_constant():
    cos, sin = tables()
    out = np.zeros((REACH, 4, 2, 4, GRID), np.float64)
    for k in range(1, REACH + 1):
        for y in range(4):
            out[k - 1, y, 0, y] = cos[:, k]
            out[k - 1, y, 1, y] = -sin[:, k]
    return out.reshape(REACH * 8, 4 * GRID)


def y_spans():
    cols = columns()
    spans = []
    for start in range(0, COLS, TILE):
        ks = [k for _, k in cols[start : start + TILE]]
        spans.append((min(ks) - 1, max(ks)))
    return spans


def y_constant():
    cos, sin = tables()
    out = np.zeros((2, GRID, 2, TILE), np.float64)
    for q in range(-REACH, REACH + 1):
        out[0, :, 0, q + REACH] = cos[:, q % GRID]
        out[0, :, 1, q + REACH] = sin[:, q % GRID]
        out[1, :, 0, q + REACH] = -sin[:, q % GRID]
        out[1, :, 1, q + REACH] = cos[:, q % GRID]
    return out.reshape(2, 2 * GRID, TILE)


def y_runs():
    cols = columns()
    runs = []
    for tile, (first, last) in enumerate(y_spans()):
        own = cols[tile * TILE : (tile + 1) * TILE]
        for k in range(first + 1, last + 1):
            lanes = [lane for lane, col in enumerate(own) if col[1] == k]
            q = own[lanes[0]][0]
            runs.append((lanes[0], lanes[-1] + 1, (q + REACH) % GRID))
    return runs


def x_constant():
    cos, sin = tables()
    out = np.zeros((2, PAIR_ROWS, GRID // 2, 2, 2, 2), np.float64)
    for pair in range(2):
        for a in range(-REACH, REACH + 1):
            c = cos[:, a % GRID].reshape(-1, 2)
            s = sin[:, a % GRID].reshape(-1, 2)
            out[pair, a + REACH, :, 0, pair] = c
            out[pair, a + REACH, :, 1, pair] = s
            out[pair, SIDE + a + REACH, :, 0, pair] = -s
            out[pair, SIDE + a + REACH, :, 1, pair] = c
    return out.reshape(2 * PAIR_ROWS, 4 * GRID)


def column_keys():
    keys = np.full((COLS, 1), -1, np.int32)
    for lane, (q, k) in enumerate(columns()):
        keys[lane, 0] = q * GRID + k
    return keys


def transform_kernel(
    val_hbm, cond_hbm, vi_hbm, ci_hbm, yq_hbm, zt_hbm, out_ref,
    val_ref, cond_ref, vi_ref, ci_ref, yq_ref, zt_ref, yt_ref, dens_ref, part_ref, sems,
):
    pairs = dens_ref.shape[0] // 2
    moves = [
        pltpu.make_async_copy(src, dst, sems.at[i])
        for i, (src, dst) in enumerate(
            (
                (yq_hbm, yq_ref),
                (val_hbm, val_ref),
                (cond_hbm, cond_ref),
                (vi_hbm, vi_ref),
                (ci_hbm, ci_ref),
                (zt_hbm, zt_ref),
            )
        )
    ]
    for move in moves:
        move.start()
    moves[0].wait()
    lane = lax.broadcasted_iota(jnp.int32, (2 * GRID, TILE), 1)
    for i, (first, last, place) in enumerate(y_runs()):
        inside = (lane >= first) & (lane < last)
        for out in range(2):
            moved = pltpu.roll(yq_ref[out], (first - place) % TILE, 1)
            yt_ref[2 * GRID * i : 2 * GRID * (i + 1), out * TILE : (out + 1) * TILE] = jnp.where(
                inside, moved, 0.0
            ).astype(BF16)
    first_pair = (
        (lax.axis_index("x") * 2 + lax.axis_index("z_lo")) * 2 + lax.axis_index("core")
    ) * pairs
    for move in moves[1:]:
        move.wait()
    for p in range(pairs):
        val = val_ref[vi_ref[first_pair + p]]
        cond = cond_ref[ci_ref[first_pair + p]]
        dens_ref[2 * p : 2 * p + 2, :] = val * cond
    for j in range(GRID // 4):
        zt = lax.dot_general(
            zt_ref[...],
            dens_ref[:, j * 256 : (j + 1) * 256],
            (((1,), (1,)), ((), ())),
            preferred_element_type=F32,
        )
        part_ref[:, j * 8 : (j + 1) * 8, :] = zt.reshape(REACH, 8, 2 * pairs)
    low = lax.broadcasted_iota(jnp.int32, (2 * pairs, TILE), 0) % 8 < 4
    row = 0
    for tile, (first, last) in enumerate(y_spans()):
        depth = (last - first) * 2 * GRID
        left = part_ref[first:last].astype(BF16).reshape(depth, 2 * pairs)
        both = lax.dot_general(
            left, yt_ref[row : row + depth, :], (((0,), (0,)), ((), ())), preferred_element_type=F32
        )
        row += depth
        real, imag = both[:, :TILE], both[:, TILE:]
        even = jnp.where(low, real, pltpu.roll(imag, 4, 0))
        odd = jnp.where(low, pltpu.roll(real, 2 * pairs - 4, 0), imag)
        for m in range(2 * pairs // 8):
            out_ref[16 * m : 16 * m + 16, tile * TILE : (tile + 1) * TILE] = jnp.concatenate(
                [even[8 * m : 8 * m + 8], odd[8 * m : 8 * m + 8]], 0
            ).astype(BF16)


def transform(pairs, val_index, cond_index, val_orbitals, cond_orbitals):
    hbm = pl.BlockSpec(memory_space=pltpu.HBM)
    y_table = jnp.asarray(jnp.asarray(y_constant(), BF16), F32)
    z_table = jnp.asarray(z_constant(), BF16)
    return pl.pallas_call(
        transform_kernel,
        out_shape=jax.ShapeDtypeStruct((4 * pairs, COLS), BF16),
        in_specs=[hbm] * 6,
        out_specs=pl.BlockSpec(memory_space=pltpu.VMEM),
        scratch_shapes=[
            pltpu.VMEM(val_orbitals.shape, BF16),
            pltpu.VMEM(cond_orbitals.shape, BF16),
            pltpu.SMEM(val_index.shape, jnp.int32),
            pltpu.SMEM(cond_index.shape, jnp.int32),
            pltpu.VMEM(y_table.shape, F32),
            pltpu.VMEM(z_table.shape, BF16),
            pltpu.VMEM((len(y_runs()) * 2 * GRID, 2 * TILE), BF16),
            pltpu.VMEM((2 * pairs, GRID * GRID), BF16),
            pltpu.VMEM((REACH, 2 * GRID, 2 * pairs), F32),
            pltpu.SemaphoreType.DMA((6,)),
        ],
        compiler_params=pltpu.CompilerParams(vmem_limit_bytes=VMEM_LIMIT),
        name="transform",
    )(val_orbitals, cond_orbitals, val_index, cond_index, y_table, z_table)


def select_kernel(y_ref, xt_ref, key_ref, gmap_ref, out_ref):
    spec = jnp.dot(xt_ref[...], y_ref[...], preferred_element_type=F32)
    spec = (spec * float(GRID) ** (-1.5)).astype(BF16)
    rows, _, width = gmap_ref.shape
    half = width // 2
    side = lax.broadcasted_iota(jnp.int32, (PAIR_ROWS, width), 0)
    for r in range(rows):
        entry = gmap_ref[r]
        key = entry & (GRID * GRID - 1)
        wave_a = (entry >> 12) & (GRID - 1)
        row = (entry >> 18) * SIDE + ((wave_a + REACH) & (GRID - 1))
        same = key_ref[...].astype(jnp.int16) == key.astype(jnp.int16)
        hit = jnp.where(same, jnp.asarray(1, BF16), jnp.asarray(0, BF16))
        found = jnp.dot(spec, hit, preferred_element_type=F32)
        here = side == row
        picked = [
            jnp.sum(jnp.where(here, found[i * PAIR_ROWS : (i + 1) * PAIR_ROWS], 0.0), 0, keepdims=True)
            for i in range(2)
        ]
        both = jnp.concatenate(picked, 0).astype(BF16)
        halves = both[:, :half], both[:, half:]
        for col in range(2 * rows):
            out_ref[r * 2 * rows + col, :, :half] = halves[col % 2]
        for which in range(2):
            col = 2 * r + which
            for other in range(rows):
                third = other % 2 if other // 2 % 2 == 0 else 2
                out_ref[other * 2 * rows + col, :, half:] = halves[which][
                    :, third * TILE : (third + 1) * TILE
                ]


def select(block, gmap, rows):
    width = NG // rows
    vmem = pl.BlockSpec(memory_space=pltpu.VMEM)
    return pl.pallas_call(
        select_kernel,
        out_shape=jax.ShapeDtypeStruct((2 * rows * rows, 2, width // 2 + TILE), BF16),
        in_specs=[vmem] * 4,
        out_specs=vmem,
        compiler_params=pltpu.CompilerParams(vmem_limit_bytes=32 * 2**20),
        name="select",
    )(block, jnp.asarray(x_constant(), BF16), jnp.asarray(column_keys()), gmap.reshape(rows, 1, width))


def product_kernel(
    mine_ref, low_ref, high_ref, zs_ref, cores_ref, weight_ref, out_ref, right_ref, res_ref, sems
):
    pairs = right_ref.shape[0]
    half = mine_ref.shape[2] - TILE
    freqs = weight_ref.shape[0]
    for third, value in enumerate((cores_ref[0], cores_ref[1], zs_ref[1])):
        right_ref[:, third * TILE : (third + 1) * TILE] = value.reshape(pairs, TILE)
    right = right_ref[...]
    own = lax.axis_index("y") % 2
    moves = []
    for step in range(2):
        if step == 0:
            left = mine_ref[:, :, :half].reshape(pairs, half)
        else:
            part = (pairs // 2, half)
            left = jnp.concatenate([low_ref[...].reshape(part), high_ref[...].reshape(part)], 0)
        place = own if step == 0 else 1 - own
        place = pl.ds(pl.multiple_of(place * half, half), half)
        turned = left.T.astype(F32)
        for f in range(freqs):
            weighted = (turned * weight_ref[f : f + 1, :]).astype(BF16)
            total = jnp.dot(weighted, right, preferred_element_type=F32)
            res_ref[step, f] = total * (1.0 / math.sqrt(pairs))
            moves.append(
                pltpu.make_async_copy(
                    res_ref.at[step, f], out_ref.at[f, place], sems.at[step * freqs + f]
                )
            )
            moves[-1].start()
    for move in moves:
        move.wait()


def product(mine, low, high, by_z, by_core, weights, rows, width):
    freqs = weights.shape[0]
    return pl.pallas_call(
        product_kernel,
        out_shape=jax.ShapeDtypeStruct((freqs, rows, width), F32),
        in_specs=[pl.BlockSpec(memory_space=pltpu.VMEM)] * 6,
        out_specs=pl.BlockSpec(memory_space=pltpu.HBM),
        scratch_shapes=[
            pltpu.VMEM((PAIRS, width), BF16),
            pltpu.VMEM((2, freqs, rows // 2, width), F32),
            pltpu.SemaphoreType.DMA((2 * freqs,)),
        ],
        compiler_params=pltpu.CompilerParams(vmem_limit_bytes=32 * 2**20),
        name="product",
    )(mine, low, high, by_z, by_core, weights)


def pair_weights(val_index, cond_index, val_energy, cond_energy, freqs):
    val_hit = val_index[:, None] == jnp.arange(val_energy.shape[0], dtype=jnp.int32)[None, :]
    cond_hit = cond_index[:, None] == jnp.arange(cond_energy.shape[0], dtype=jnp.int32)[None, :]
    gap = jnp.sum(jnp.where(cond_hit, cond_energy[None, :], 0.0), 1) - jnp.sum(
        jnp.where(val_hit, val_energy[None, :], 0.0), 1
    )
    return -4.0 * gap[None, :] / (gap[None, :] ** 2 + freqs[:, None] ** 2)


ROW = ("x", "z_lo", "core")
COL = ("z_hi", "y")


def shards(
    val_orbitals, cond_orbitals, val_index, cond_index, val_energy, cond_energy, freqs, gmap
):
    row_count = lax.axis_size(ROW)
    col_count = lax.axis_size(COL)
    pair_dev = val_index.shape[0] // row_count
    partial = transform(pair_dev, val_index, cond_index, val_orbitals, cond_orbitals)
    block = lax.all_to_all(
        partial.reshape(col_count, 8, COLS), COL, split_axis=0, concat_axis=0, tiled=True
    ).reshape(4 * GRID, COLS)
    weights = pair_weights(val_index, cond_index, val_energy, cond_energy, freqs)
    block, weights = lax.optimization_barrier((block, weights))
    mine = lax.all_to_all(
        select(block, gmap, row_count), ROW + COL, split_axis=0, concat_axis=0, tiled=True
    )
    sources = mine.shape[0] // 2
    rows, width = NG // row_count, NG // col_count
    half = rows // 2
    count = lax.axis_size("y")
    low = lax.ppermute(mine[:sources, :, :half], "y", [((i + 1) % count, i) for i in range(count)])
    high = lax.ppermute(mine[sources:, :, :half], "y", [(i, (i + 1) % count) for i in range(count)])
    by_z = lax.all_gather(mine[:, :, half:], "z_lo")
    by_core = lax.all_gather(by_z[0], "core")
    return product(mine, low, high, by_z, by_core, weights, rows, width)


def solution(mesh):
    fine = Mesh(mesh.devices.reshape(4, 2, 2, 4, 8), ROW + COL)
    orbitals = P(None, COL, None)
    placed = (orbitals, orbitals, P(), P(), P(), P(), P(), P())
    return jax.shard_map(
        shards, mesh=fine, in_specs=placed, out_specs=P(None, ROW, COL), check_vma=False
    )
```
